128 devices in a mesh: cyl: 4 (over z_lo, core), scen: 32 (over y, x, z_hi).
Axes of the slice: x: 4, y: 4, z: 4 (z_hi: 2, z_lo: 2; z = z_hi * 2 + z_lo), core: 2. Of those that a mesh axis runs over, the one named last changes fastest.
Arguments:
- costs: float32 [2048, 20480], P('scen'), may hold values from -6 to 6
- rhs: float32 [2048, 4096], P('scen'), may hold values from -6 to 6
- multipliers: float32 [2048, 16384], P('scen'), may hold values from -4 to 4
- xbar_first_in: float32 [8192], replicated, may hold values from 0 to 1
- xbar_node_in: float32 [48, 8192], replicated, may hold values from 0 to 1
- prox_weights: float32 [4], replicated, may hold values from 0.5 to 4
- start_primal: float32 [2048, 20480], P('scen'), may hold values from 0 to 1
- start_dual: float32 [2048, 4096], P('scen'), may hold values from 0 to 1
- recourse_blocks: bfloat16 [32, 3, 128, 128], replicated, may hold values from -0.3125 to 0.3125
- block_pattern: int32 [32, 3], replicated, may hold values from 0 to 159, as said below
- node_of: int32 [2048], P('scen'), may hold values from 0 to 47, as said below
- pdhg_counts: int32 [4, 2048], P('cyl', 'scen'), may hold values from 3 to 6, as said below
Outputs:
- primal: float32 [4, 2048, 20480], P('cyl', 'scen')
- dual: float32 [4, 2048, 4096], P('cyl', 'scen')
- xbar_first: float32 [8192], replicated
- xbar_node: float32 [48, 8192], replicated
- new_multipliers: float32 [2048, 16384], P('scen')
- objectives: float32 [4], replicated
The draws below stay inside these ranges and needn't reach their ends.
Inputs may be any that keep to these rules, and one draw needn't show every extreme that they name: `block_pattern`: block column 0 of block row r is 128 + r mod (32); the other 2 of a row are distinct block columns below 128. `node_of`: every node has at least one scenario. `pdhg_counts`: some entry equals 6.
All inputs are finite; a program needn't handle non-finite values.
Results may differ from the reference program's by a relative error of at most 0.00081.
Values sent between devices are 32-bit elements; how exact they have to be, the bound alone decides.
No kernel may reach another device: no remote copies, remote signals or barrier semaphores. Data moves between devices by JAX's collectives and lax.ppermute only.
A program may use at most 128 MiB of HBM per device.

```python
import math
import jax
import jax.numpy as jnp
from jax import lax

N1 = 8192
N2 = 8192
NNA = 16384
M = 4096
NY = 4096
NZ = 20480
BLK = 128
K = 3
RB = 32
CB = 160
Q = 96
NODES = 48
S_DEV = 64
SCEN = 2048
ITER_MIN = 3
ITER_MAX = 6
N_CYL = 4


def draw_block_pattern(key, part):
    key = jax.random.fold_in(key, 11)
    rows = jnp.arange(RB, dtype=jnp.int32)
    own = NNA // BLK + rows % (NY // BLK)
    keys = jax.random.split(key, RB)
    others = jax.vmap(lambda one: jax.random.permutation(one, NNA // BLK)[:K - 1])(keys)
    return jnp.concatenate([own[:, None], others.astype(jnp.int32)], axis=1)


def draw_node_of(key, part):
    key = jax.random.fold_in(key, 12)
    first, second = jax.random.split(key)
    places = jnp.arange(SCEN, dtype=jnp.int32)
    spread = jax.random.randint(first, (SCEN,), 0, NODES, dtype=jnp.int32)
    base = jnp.where(places < NODES, places, spread)
    return jax.random.permutation(second, base).astype(jnp.int32)


def draw_pdhg_counts(key, part):
    key = jax.random.fold_in(key, 13)
    first, second = jax.random.split(key)
    groups = SCEN // S_DEV
    limit = jax.random.randint(first, (N_CYL, groups), ITER_MIN, ITER_MAX + 1, dtype=jnp.int32)
    limit = limit.at[0, 0].set(ITER_MAX)
    limit_rows = jnp.repeat(limit, S_DEV, axis=1)
    counts = jax.random.randint(second, (N_CYL, SCEN), ITER_MIN, limit_rows + 1, dtype=jnp.int32)
    return counts.at[0, 0].set(ITER_MAX).astype(jnp.int32)


def steps_of(key, dims, shards, least, top_value):
    def one(dim, parts):
        heights = jax.random.uniform(jax.random.fold_in(jax.random.fold_in(key, 6), dim), (parts,), jnp.float32, least / len(shards), top_value / len(shards))
        return jnp.repeat(jnp.exp(heights), dims[dim] // parts).reshape((-1,) + (1,) * (len(dims) - dim - 1))

    level = one(*shards[0])
    for cut in shards[1:]:
        level = level * one(*cut)
    return level


def scatter_about(own_key, shape, width, most, cuts=(), kind=jnp.bfloat16):
    gain = steps_of(own_key, shape, cuts, -0.22, 0.18) if cuts else 1.0
    array = jax.random.normal(own_key, shape, jnp.float32) * width * gain
    return jnp.minimum(jnp.maximum(array, -most), most).astype(kind)


def setup_inputs(seed: int = 0) -> dict:
    key_of = jax.random.split(jax.random.key(seed), 13)
    costs = scatter_about(key_of[0], (SCEN, NZ), 1.0, 6.0, ((0, 32),), jnp.float32)
    rhs = scatter_about(key_of[1], (SCEN, M), 1.0, 6.0, ((0, 32),), jnp.float32)
    multipliers = scatter_about(key_of[2], (SCEN, NNA), 0.5, 4.0, ((0, 32),), jnp.float32)
    xbar_first_in = jnp.clip(jax.random.uniform(key_of[3], (N1,), jnp.float32, 0.0, 1.0), 0.0, 1.0)
    xbar_node_in = jnp.clip(jax.random.uniform(key_of[4], (NODES, N2), jnp.float32, 0.0, 1.0), 0.0, 1.0)
    prox_weights = jnp.clip(jnp.exp(jax.random.uniform(key_of[5], (N_CYL,), jnp.float32, math.log(0.5), math.log(4.0))), 0.5, 4.0)
    start_primal = jnp.clip(1.0 * jax.random.uniform(key_of[6], (SCEN, NZ), jnp.float32) ** steps_of(key_of[6], (SCEN, NZ), ((0, 32),), -0.2, 0.2), 0.0, 1.0)
    start_dual = jnp.clip(1.0 * jax.random.uniform(key_of[7], (SCEN, M), jnp.float32) ** steps_of(key_of[7], (SCEN, M), ((0, 32),), -0.2, 0.2), 0.0, 1.0)
    recourse_blocks = scatter_about(key_of[8], (RB, K, BLK, BLK), (K * BLK) ** -0.5, 0.3125)
    block_pattern = draw_block_pattern(jax.random.fold_in(key_of[12], 71), 0)
    node_of = draw_node_of(jax.random.fold_in(key_of[12], 71), 0)
    pdhg_counts = draw_pdhg_counts(jax.random.fold_in(key_of[12], 71), 0)
    return dict(costs=costs, rhs=rhs, multipliers=multipliers, xbar_first_in=xbar_first_in, xbar_node_in=xbar_node_in, prox_weights=prox_weights, start_primal=start_primal, start_dual=start_dual, recourse_blocks=recourse_blocks, block_pattern=block_pattern, node_of=node_of, pdhg_counts=pdhg_counts)


TAU = 0.4
SIGMA = 0.4


def apply_blocks(ext, recourse_blocks, block_pattern):
    count = ext.shape[0]
    cols = block_pattern.reshape(-1).astype(jnp.int32)
    tiles = jnp.take(ext.reshape(count, CB, BLK), cols, axis=1)
    flat = recourse_blocks.reshape(Q, BLK, BLK)
    out = jnp.einsum('sqj,qij->sqi', tiles.astype(jnp.float32), flat.astype(jnp.float32))
    return out.reshape(count, RB, K, BLK).sum(axis=2).reshape(count, M)


def apply_transpose(dual_low, recourse_blocks, block_pattern):
    count = dual_low.shape[0]
    cols = block_pattern.reshape(-1).astype(jnp.int32)
    spread = jnp.broadcast_to(dual_low.reshape(count, RB, 1, BLK), (count, RB, K, BLK)).reshape(count, Q, BLK)
    flat = recourse_blocks.reshape(Q, BLK, BLK)
    contrib = jnp.einsum('sqi,qij->sqj', spread.astype(jnp.float32), flat.astype(jnp.float32))
    total = jnp.zeros((count, CB, BLK), jnp.float32).at[:, cols, :].add(contrib)
    return total.reshape(count, NZ)


def reference(costs, rhs, multipliers, xbar_first_in, xbar_node_in, prox_weights, start_primal, start_dual, recourse_blocks, block_pattern, node_of, pdhg_counts):
    gradient = costs + jnp.concatenate([multipliers, jnp.zeros((SCEN, NY), jnp.float32)], axis=1)
    target = jnp.concatenate([jnp.broadcast_to(xbar_first_in[None, :], (SCEN, N1)), jnp.take(xbar_node_in, node_of, axis=0), jnp.zeros((SCEN, NY), jnp.float32)], axis=1)
    mask = (jnp.arange(NZ) < NNA).astype(jnp.float32)
    primals = []
    duals = []
    for cylinder in range(N_CYL):
        rho_vec = prox_weights[cylinder] * mask
        counts = pdhg_counts[cylinder]

        def turn(step, state):
            primal_now, dual_now = state
            back = apply_transpose(dual_now.astype(jnp.bfloat16), recourse_blocks, block_pattern)
            fresh = jnp.clip((primal_now - TAU * (gradient - back) + TAU * rho_vec * target) / (1.0 + TAU * rho_vec), 0.0, 1.0)
            ext = (2.0 * fresh - primal_now).astype(jnp.bfloat16)
            image = apply_blocks(ext, recourse_blocks, block_pattern)
            dual_new = jnp.maximum(0.0, dual_now + SIGMA * (rhs - image))
            live = (step < counts)[:, None]
            return jnp.where(live, fresh, primal_now), jnp.where(live, dual_new, dual_now)

        primal_end, dual_end = lax.fori_loop(0, ITER_MAX, turn, (start_primal, start_dual))
        primals.append(primal_end)
        duals.append(dual_end)
    hub = primals[0][:, :NNA]
    xbar_first = jnp.sum(hub[:, :N1], axis=0) / SCEN
    tally = jax.ops.segment_sum(jnp.ones((SCEN,), jnp.float32), node_of, NODES)
    node_sums = jax.ops.segment_sum(hub[:, N1:], node_of, NODES)
    xbar_node = node_sums / tally[:, None]
    average = jnp.concatenate([jnp.broadcast_to(xbar_first[None, :], (SCEN, N1)), jnp.take(xbar_node, node_of, axis=0)], axis=1)
    new_multipliers = multipliers + prox_weights[0] * (hub - average)
    objectives = []
    for cylinder in range(N_CYL):
        value = jnp.sum(costs * primals[cylinder]) + jnp.sum(new_multipliers * primals[cylinder][:, :NNA])
        objectives.append(value / SCEN)
    return jnp.stack(primals), jnp.stack(duals), xbar_first, xbar_node, new_multipliers, jnp.stack(objectives)
```

```python
import functools

import jax
import jax.numpy as jnp
from jax import lax
from jax.experimental import pallas as pl
from jax.experimental.pallas import tpu as pltpu
from jax.sharding import PartitionSpec as P

N1 = 8192
N2 = 8192
NNA = 16384
M = 4096
NZ = 20480
BLK = 128
RB = 32
Q = 96
NODES = 48
SCEN = 2048
ROWS = 64
N_CYL = 4
GROUPS = 32
HALF = 24
SHARD = 32
CB1 = N1 // BLK
CBA = NNA // BLK
CHUNK = 2048
PER = CHUNK // BLK
ZERO_SLOT = 96
ALL = ("scen", "cyl")

TAU = 0.4
SIGMA = 0.4

ANY = pl.BlockSpec(memory_space=pl.ANY)
VM = pl.BlockSpec(memory_space=pltpu.VMEM)
SM = pl.BlockSpec(memory_space=pltpu.SMEM)


def cols(c):
    return pl.ds(pl.multiple_of(c * BLK, BLK), BLK)


def split(value):
    high = value.astype(jnp.bfloat16)
    return high, (value - high.astype(jnp.float32)).astype(jnp.bfloat16)


def dot(a, b):
    return jnp.dot(a, b, preferred_element_type=jnp.float32)


def one_hot(node_ref):
    lanes = lax.broadcasted_iota(jnp.int32, (ROWS, BLK), 1)
    return (node_ref[...] == lanes).astype(jnp.float32)


def solve_kernel(
    pattern, prox, costs, rhs, mult, first_in, node_in, start, start_dual, blocks, node_rows, counts,
    primal, dual, weights, sums, cost_sum,
    head, coupled, slot, free, dup_to, dup_from,
    z, d, gc, gm, back, ext, u, uq, rh, raw, wide, tall, nodes, firsts, shards,
    sem, osem,
):
    cyl = lax.axis_index("cyl")
    rhos = (prox[0], prox[cyl])
    invs = [1.0 / (1.0 + TAU * jnp.full((8, BLK), rho, jnp.float32)) for rho in rhos]
    inv = [jnp.broadcast_to(one[:1], (ROWS, BLK)) for one in invs]
    coef = [TAU * one for one in inv]
    pull = [TAU * rho * one for rho, one in zip(rhos, inv)]
    part = [slice(0, ROWS), slice(ROWS, 2 * ROWS)]

    def copy(src, dst, k):
        return pltpu.make_async_copy(src, dst, sem.at[k])

    block_copy = copy(blocks, raw, 0)
    dual_copies = [copy(start_dual, u.at[part[g]], 1 + g) for g in range(2)]
    node_copy = copy(node_in, nodes, 3)
    first_copy = copy(first_in, firsts, 4)
    rhs_copy = copy(rhs, rh, 5)
    chunk_copies = []
    for n in range(NZ // CHUNK):
        at = pl.ds(n * CHUNK, CHUNK)
        group = [copy(costs.at[:, at], gc.at[:, at], 6 + 4 * n)]
        if n * CHUNK < NNA:
            group.append(copy(mult.at[:, at], gm.at[:, at], 7 + 4 * n))
        for g in range(2):
            group.append(copy(start.at[:, at], z.at[part[g], at], 8 + 4 * n + g))
        chunk_copies.append(group)
    for one in [block_copy, *dual_copies, *sum(chunk_copies[NNA // CHUNK:], []), node_copy, first_copy]:
        one.start()
    for group in chunk_copies[: NNA // CHUNK]:
        for one in group:
            one.start()
    rhs_copy.start()

    def clear(c, carry):
        slot[c] = -1
        return carry

    lax.fori_loop(0, CBA, clear, 0, unroll=8)

    def note(r, dups):
        for k in range(2):
            c = pattern[r, k + 1]
            s = 2 * r + k
            was = slot[c]
            seen = (was >= 0).astype(jnp.int32)
            lead = jnp.where(was >= 0, was, s)
            slot[c] = lead
            head[s] = lead
            dup_to[dups] = lead
            dup_from[dups] = s
            dups = dups + seen
        return dups

    dups = lax.fori_loop(0, RB, note, 0)

    def place(c, carry):
        used, unused = carry
        was = slot[c]
        hit = (was >= 0).astype(jnp.int32)
        coupled[used] = c
        slot[CBA + used] = was
        free[unused] = c
        return used + hit, unused + 1 - hit

    used, _ = lax.fori_loop(0, CBA, place, (0, 0), unroll=4)

    def fill(j, carry):
        coupled[j] = free[64 + j - used]
        slot[CBA + j] = ZERO_SLOT
        return carry

    lax.fori_loop(used, 64, fill, 0)

    back[:, cols(ZERO_SLOT)] = jnp.zeros((2 * ROWS, BLK), jnp.float32)
    block_copy.wait()

    def arrange(r, carry):
        for k in range(3):
            one = raw[3 * r + k]
            wide[r, :, k * BLK : (k + 1) * BLK] = one
            tall[r, k * BLK : (k + 1) * BLK, :] = one.T
        return carry

    lax.fori_loop(0, RB, arrange, 0, unroll=4)
    for one in dual_copies:
        one.wait()

    def low_dual(r, carry):
        uq[:, cols(r)] = u[:, cols(r)].astype(jnp.bfloat16)
        return carry

    lax.fori_loop(0, RB, low_dual, 0, unroll=4)
    for one in sum(chunk_copies[NNA // CHUNK:], []):
        one.wait()

    def pick(g, t, new, old):
        if t is None:
            return new
        return jnp.where(counts[part[g], :] > t, new, old)

    def spread(t):
        for r in range(RB):
            product = dot(uq[:, r * BLK : (r + 1) * BLK], wide[r])
            back[:, 2 * r * BLK : (2 * r + 2) * BLK] = product[:, BLK:]
            at = slice(NNA + r * BLK, NNA + (r + 1) * BLK)
            for g in range(2):
                now = z[part[g], at]
                fresh = jnp.clip(now + TAU * (product[part[g], :BLK] - gc[:, at]), 0.0, 1.0)
                ext[part[g], (64 + r) * BLK : (65 + r) * BLK] = (fresh + fresh - now).astype(jnp.bfloat16)
                z[part[g], at] = pick(g, t, fresh, now)

        def merge(k, carry):
            to = cols(dup_to[k])
            back[:, to] += back[:, cols(dup_from[k])]
            return carry

        lax.fori_loop(0, dups, merge, 0)

    def touch(t):
        def step(j, carry):
            c = cols(coupled[j])
            s = cols(slot[CBA + j])
            for g in range(2):
                now = z[part[g], c]
                fresh = jnp.clip(now * inv[g] + back[part[g], s] * coef[g] + d[part[g], c], 0.0, 1.0)
                ext[part[g], s] = (fresh + fresh - now).astype(jnp.bfloat16)
                z[part[g], c] = pick(g, t, fresh, now)
            return carry

        lax.fori_loop(0, 64, step, 0, unroll=8)

    def image(t):
        for r in range(RB):
            at = slice(r * BLK, (r + 1) * BLK)
            left = [ext[:, (64 + r) * BLK : (65 + r) * BLK], ext[:, cols(head[2 * r])], ext[:, cols(head[2 * r + 1])]]
            product = dot(jnp.concatenate(left, axis=1), tall[r])
            for g in range(2):
                old = u[part[g], at]
                new = jnp.maximum(0.0, old + SIGMA * (rh[:, at] - product[part[g]]))
                new = pick(g, t, new, old)
                u[part[g], at] = new
                uq[part[g], at] = new.astype(jnp.bfloat16)

    spread(None)
    node_copy.wait()
    first_copy.wait()
    hot = one_hot(node_rows)
    hot_low = hot.astype(jnp.bfloat16)[:, :NODES]
    for n in range(NNA // CHUNK):
        for one in chunk_copies[n]:
            one.wait()

        def prepare(c, carry):
            if n * CHUNK < N1:
                target = jnp.broadcast_to(firsts[pl.ds(c, 1), :], (ROWS, BLK))
            else:
                high, low = split(nodes[:, cols(c - CB1)])
                target = dot(hot_low, high) + dot(hot_low, low)
            gradient = gc[:, cols(c)] + gm[:, cols(c)]
            for g in range(2):
                d[part[g], cols(c)] = pull[g] * target - coef[g] * gradient
            return carry

        lax.fori_loop(n * PER, (n + 1) * PER, prepare, 0, unroll=4)
    rhs_copy.wait()

    def plain(t, carry):
        touch(None)
        image(None)
        spread(None)
        return carry

    def chosen(t, carry):
        touch(t)
        image(t)
        spread(t + 1)
        return carry

    lax.fori_loop(0, 2, plain, 0)
    lax.fori_loop(2, 5, chosen, 0)
    touch(5)

    def loose(j, carry):
        c = cols(free[j])
        for g in range(2):
            now = z[part[g], c]
            shift = d[part[g], c]
            for t in range(6):
                fresh = jnp.clip(now * inv[g] + shift, 0.0, 1.0)
                now = pick(g, t if t > 2 else None, fresh, now)
            z[part[g], c] = now
        return carry

    lax.fori_loop(0, 64, loose, 0, unroll=2)

    def send(src, dst, k):
        one = pltpu.make_async_copy(src, dst, osem.at[k])
        one.start()
        return one

    outs = [send(z.at[part[1]], primal.at[0], 0)]
    image(5)
    outs.append(send(u.at[part[1]], dual.at[0], 1))

    hot_turned = hot.T[:NODES].astype(jnp.bfloat16)
    tally = jnp.sum(hot, axis=0, keepdims=True)

    def shard(m, carry):
        block = cyl * PER + m
        high, low = split(z[part[0], cols(CB1 + block)])
        node_sum = dot(hot_turned, high) + dot(hot_turned, low)
        first_sum = jnp.sum(z[part[0], cols(block)], axis=0, keepdims=True)
        tail = jnp.concatenate([first_sum, tally, jnp.zeros((SHARD - HALF - 2, BLK), jnp.float32)], axis=0)
        for half in range(2):
            shards[2 * m + half, :HALF, :] = node_sum[half * HALF : (half + 1) * HALF]
            shards[2 * m + half, HALF:, :] = tail
        return carry

    lax.fori_loop(0, PER, shard, 0, unroll=2)
    outs.append(send(shards, sums, 2))

    hub_rho = rhos[0]
    for n in range(NNA // CHUNK):
        at = slice(n * CHUNK, (n + 1) * CHUNK)
        gm[:, at] = gm[:, at] + hub_rho * z[part[0], at]
        outs.append(send(gm.at[:, at], weights.at[:, at], 3 + n))
    total = jnp.zeros((ROWS, BLK), jnp.float32)

    def cost(c, acc):
        return acc + gc[:, cols(c)] * z[part[1], cols(c)]

    total = lax.fori_loop(0, NZ // BLK, cost, total, unroll=4)
    cost_sum[...] = jnp.sum(total.reshape(ROWS // 8, 8, BLK), axis=0)
    for one in outs:
        one.wait()


def solve(pattern, prox, costs, rhs, mult, first_in, node_in, start, start_dual, blocks, node_rows, counts):
    f32, bf16 = jnp.float32, jnp.bfloat16
    both = 2 * ROWS
    V = pltpu.VMEM
    return pl.pallas_call(
        solve_kernel,
        out_shape=[
            jax.ShapeDtypeStruct((1, ROWS, NZ), f32),
            jax.ShapeDtypeStruct((1, ROWS, M), f32),
            jax.ShapeDtypeStruct((ROWS, NNA), f32),
            jax.ShapeDtypeStruct((GROUPS, SHARD, BLK), f32),
            jax.ShapeDtypeStruct((8, BLK), f32),
        ],
        in_specs=[SM, SM] + [ANY] * 8 + [VM, VM],
        out_specs=[ANY] * 4 + [VM],
        scratch_shapes=[
            pltpu.SMEM((72,), jnp.int32),
            pltpu.SMEM((136,), jnp.int32),
            pltpu.SMEM((2 * CBA + 8,), jnp.int32),
            pltpu.SMEM((136,), jnp.int32),
            pltpu.SMEM((72,), jnp.int32),
            pltpu.SMEM((72,), jnp.int32),
            V((both, NZ), f32),
            V((both, NNA), f32),
            V((ROWS, NZ), f32),
            V((ROWS, NNA), f32),
            V((both, 97 * BLK), f32),
            V((both, 97 * BLK), bf16),
            V((both, M), f32),
            V((both, M), bf16),
            V((ROWS, M), f32),
            V((Q, BLK, BLK), bf16),
            V((RB, BLK, 3 * BLK), bf16),
            V((RB, 3 * BLK, BLK), bf16),
            V((NODES, N2), f32),
            V((CB1, BLK), f32),
            V((GROUPS, SHARD, BLK), f32),
            pltpu.SemaphoreType.DMA((48,)),
            pltpu.SemaphoreType.DMA((12,)),
        ],
        compiler_params=pltpu.CompilerParams(vmem_limit_bytes=62 * 2**20),
        name="solve",
    )(pattern, prox, costs, rhs, mult, first_in, node_in, start, start_dual, blocks, node_rows, counts)


def average_kernel(sums, out):
    half = lax.axis_index("scen") % 2
    total = sums[0]
    for i in range(1, GROUPS):
        total = total + sums[i]
    tally = jnp.broadcast_to(total[HALF + 1 : HALF + 2], (HALF, BLK))
    lanes = lax.broadcasted_iota(jnp.int32, (HALF, BLK), 1)
    wanted = lax.broadcasted_iota(jnp.int32, (HALF, BLK), 0) + half * HALF
    count = jnp.sum(jnp.where(lanes == wanted, tally, 0.0), axis=1, keepdims=True)
    low = total[:HALF] / count
    rest = total[HALF:] * (1.0 / SCEN)
    top = low[: SHARD // 2]
    bottom = jnp.concatenate([low[SHARD // 2 :], rest], axis=0)

    def put(i, carry):
        for c in range(N_CYL):
            out[i * N_CYL + c] = bottom if c % 2 else top
        return carry

    lax.fori_loop(0, GROUPS, put, 0, unroll=2)


def average(sums):
    return pl.pallas_call(
        average_kernel,
        out_shape=jax.ShapeDtypeStruct((GROUPS * N_CYL, SHARD // 2, BLK), jnp.float32),
        in_specs=[VM],
        out_specs=VM,
        name="average",
    )(sums)


def update_kernel(
    prox, mine, other, weights, primal, node_rows, cost_sum,
    multipliers, first_out, node_out, value,
    shards, w, x, nodes, sem, osem,
):
    cyl = lax.axis_index("cyl")
    core = cyl % 2
    rho = prox[0]

    def copy(src, dst, k):
        return pltpu.make_async_copy(src, dst, sem.at[k])

    parts = [copy(mine, shards.at[core], 0), copy(other, shards.at[1 - core], 1)]
    for one in parts:
        one.start()
    chunks = []
    for n in range(NNA // CHUNK):
        at = pl.ds(n * CHUNK, CHUNK)
        group = [copy(weights.at[:, at], w.at[:, at], 2 + 2 * n), copy(primal.at[0, :, at], x.at[:, at], 3 + 2 * n)]
        for one in group:
            one.start()
        chunks.append(group)
    hot = one_hot(node_rows).astype(jnp.bfloat16)[:, :NODES]
    for one in parts:
        one.wait()

    outs = []
    acc = jnp.zeros((ROWS, BLK), jnp.float32)
    for n in range(NNA // CHUNK):
        for one in chunks[n]:
            one.wait()

        def step(m, acc):
            if n * CHUNK < N1:
                block = n * PER + m
                lead = 8 * m + n
                row = shards[1, lead, pl.ds(HALF - SHARD // 2, 1), :]
                first_out[pl.ds(block, 1), :] = row
                own = jnp.broadcast_to(row, (ROWS, BLK))
            else:
                lead = 8 * m + n - N1 // CHUNK
                nodes_now = jnp.concatenate(
                    [
                        shards[0, lead],
                        shards[1, lead, : HALF - SHARD // 2, :],
                        shards[0, lead + N_CYL],
                        shards[1, lead + N_CYL, : HALF - SHARD // 2, :],
                    ],
                    axis=0,
                )
                nodes[:, cols((n - N1 // CHUNK) * PER + m)] = nodes_now
                high, low = split(nodes_now)
                own = dot(hot, high) + dot(hot, low)
            c = cols(n * PER + m)
            new = w[:, c] - rho * own
            w[:, c] = new
            return acc + new * x[:, c]

        acc = lax.fori_loop(0, PER, step, acc, unroll=4)
        at = pl.ds(n * CHUNK, CHUNK)
        one = pltpu.make_async_copy(w.at[:, at], multipliers.at[:, at], osem.at[n])
        one.start()
        outs.append(one)
    one = pltpu.make_async_copy(nodes, node_out, osem.at[NNA // CHUNK])
    one.start()
    outs.append(one)
    total = jnp.sum(acc) + jnp.sum(cost_sum[...])
    value[...] = jnp.full(value.shape, total, jnp.float32)
    for one in outs:
        one.wait()


def update(prox, mine, other, weights, primal, node_rows, cost_sum):
    f32 = jnp.float32
    V = pltpu.VMEM
    return pl.pallas_call(
        update_kernel,
        out_shape=[
            jax.ShapeDtypeStruct((ROWS, NNA), f32),
            jax.ShapeDtypeStruct((CB1, BLK), f32),
            jax.ShapeDtypeStruct((NODES, N2), f32),
            jax.ShapeDtypeStruct((GROUPS * N_CYL, BLK), f32),
        ],
        in_specs=[SM, ANY, ANY, ANY, ANY, VM, VM],
        out_specs=[ANY, VM, ANY, VM],
        scratch_shapes=[
            V((2, GROUPS * N_CYL, SHARD // 2, BLK), f32),
            V((ROWS, NNA), f32),
            V((ROWS, NNA), f32),
            V((NODES, N2), f32),
            pltpu.SemaphoreType.DMA((24,)),
            pltpu.SemaphoreType.DMA((12,)),
        ],
        compiler_params=pltpu.CompilerParams(vmem_limit_bytes=40 * 2**20),
        name="update",
    )(prox, mine, other, weights, primal, node_rows, cost_sum)


def body(
    costs,
    rhs,
    multipliers,
    xbar_first_in,
    xbar_node_in,
    prox_weights,
    start_primal,
    start_dual,
    recourse_blocks,
    block_pattern,
    node_of,
    pdhg_counts,
):
    hub_counts = lax.all_gather(pdhg_counts, "cyl", axis=0, tiled=True)[0]
    counts = jnp.broadcast_to(jnp.concatenate([hub_counts, pdhg_counts[0]])[:, None], (2 * ROWS, BLK))
    node_rows = jnp.broadcast_to(node_of[:, None], (ROWS, BLK))
    primal, dual, weights, sums, cost_sum = solve(
        block_pattern,
        prox_weights,
        costs,
        rhs,
        multipliers,
        xbar_first_in.reshape(CB1, BLK),
        xbar_node_in,
        start_primal,
        start_dual,
        recourse_blocks.reshape(Q, BLK, BLK),
        node_rows,
        counts,
    )
    gathered = lax.all_to_all(sums, "scen", 0, 0, tiled=True)
    shares = average(gathered)
    mine = lax.all_to_all(shares, ALL, 0, 0, tiled=True)
    other = lax.ppermute(mine, "cyl", [(0, 1), (1, 0), (2, 3), (3, 2)])
    new_multipliers, first, xbar_node, value = update(
        prox_weights, mine, other, weights, primal, node_rows, cost_sum
    )
    values = lax.all_to_all(value, ALL, 0, 0, tiled=True)
    objectives = jnp.sum(values.reshape(GROUPS, N_CYL, BLK)[:, :, 0], axis=0) / SCEN
    return (primal, dual, first.reshape(N1), xbar_node, new_multipliers, objectives)


def solution(mesh):
    return jax.shard_map(
        body,
        mesh=mesh,
        in_specs=(
            P("scen", None),
            P("scen", None),
            P("scen", None),
            P(),
            P(),
            P(),
            P("scen", None),
            P("scen", None),
            P(),
            P(),
            P("scen"),
            P("cyl", "scen"),
        ),
        out_specs=(P("cyl", "scen", None), P("cyl", "scen", None), P(), P(), P("scen", None), P()),
        check_vma=False,
    )
```

```python
import functools

import jax
import jax.numpy as jnp
from jax import lax
from jax.experimental import pallas as pl
from jax.experimental.pallas import tpu as pltpu
from jax.sharding import PartitionSpec as P

N1 = 8192
N2 = 8192
NNA = 16384
M = 4096
NZ = 20480
BLK = 128
RB = 32
Q = 96
NODES = 48
SCEN = 2048
ROWS = 64
N_CYL = 4
GROUPS = 32
HALF = 24
SHARD = 32
CB1 = N1 // BLK
CBA = NNA // BLK
CHUNK = 2048
PER = CHUNK // BLK
ZERO_SLOT = 64
VMEM_LIMIT = 62 * 2**20
ALL = ("scen", "cyl")

TAU = 0.4
SIGMA = 0.4

ANY = pl.BlockSpec(memory_space=pl.ANY)
HBM = pl.BlockSpec(memory_space=pltpu.HBM)
VM = pl.BlockSpec(memory_space=pltpu.VMEM)
SM = pl.BlockSpec(memory_space=pltpu.SMEM)


def cols(c):
    return pl.ds(pl.multiple_of(c * BLK, BLK), BLK)


def split(value):
    high = value.astype(jnp.bfloat16)
    return high, (value - high.astype(jnp.float32)).astype(jnp.bfloat16)


def dot(a, b):
    return jnp.dot(a, b, preferred_element_type=jnp.float32)


def down(row):
    row = jnp.broadcast_to(row, (ROWS, ROWS))
    here = lax.broadcasted_iota(jnp.int32, (ROWS, ROWS), 0) == lax.broadcasted_iota(jnp.int32, (ROWS, ROWS), 1)
    return jnp.broadcast_to(jnp.sum(jnp.where(here, row, 0), axis=1, keepdims=True), (ROWS, BLK))


def one_hot(node_row):
    lanes = lax.broadcasted_iota(jnp.int32, (ROWS, BLK), 1)
    return (down(node_row) == lanes).astype(jnp.float32)


def solve_kernel(kind, *refs):
    (pattern, prox, node_of, counts_in, costs, rhs, mult, first_in, node_in, start, start_dual) = refs[:11]
    refs = refs[11:]
    is_hub = kind == "hub"
    if is_hub:
        (blocks, own_in, first_counts, second_counts, third_counts, weights, lagrange) = refs[:7]
        refs = refs[7:]
    else:
        blocks, primal, dual, sums = refs[:4]
        refs = refs[4:]
    (
        head, lead_of, coupled, slot, free, dup_to, dup_from,
        counts, z, z_odd, z_own, z_free, d, gc, gm, back, back_odd, ext, ext_own, u, uq, rh, wide, tall, nodes, firsts,
        extra, sem, osem,
    ) = (*refs[:26], refs[26:-2], *refs[-2:])
    cyl = lax.axis_index("cyl")
    rho = prox[0] if is_hub else prox[cyl]
    inv = jnp.broadcast_to((1.0 / (1.0 + TAU * jnp.full((8, BLK), rho, jnp.float32)))[:1], (ROWS, BLK))
    coef = TAU * inv
    pull = TAU * rho * inv

    def copy(src, dst, k):
        return pltpu.make_async_copy(src, dst, sem.at[k])

    block_copies = []
    for n in range(4):
        at = pl.ds(8 * n, 8)
        group = [copy(blocks.at[at, k], wide.at[at, :, pl.ds(k * BLK, BLK)], 40 + 3 * n + k) for k in range(3)]
        block_copies.append(group)
    dual_copy = copy(start_dual, u, 2)
    node_copy = copy(node_in, nodes, 3)
    first_copy = copy(first_in, firsts, 4)
    rhs_copy = copy(rhs, rh, 5)
    chunk_copies = []
    for n in range(NZ // CHUNK):
        at = pl.ds(n * CHUNK, CHUNK)
        where = z.at[:, at] if n * CHUNK < NNA else z_own.at[:, pl.ds(n * CHUNK - NNA, CHUNK)]
        group = [copy(costs.at[:, at], gc.at[:, at], 6 + 3 * n), copy(start.at[:, at], where, 7 + 3 * n)]
        if n * CHUNK < NNA:
            group.append(copy(mult.at[:, at], gm.at[:, at], 8 + 3 * n))
        chunk_copies.append(group)
    own_copies = sum(chunk_copies[NNA // CHUNK :], [])
    for one in [*sum(block_copies, []), dual_copy, *own_copies, first_copy]:
        one.start()
    for n, group in enumerate(chunk_copies[: NNA // CHUNK]):
        if n == N1 // CHUNK - 1:
            node_copy.start()
        for one in group:
            one.start()
    rhs_copy.start()
    if is_hub:
        own_copy = copy(own_in.at[0], extra[0], 0)
        own_copy.start()

    def clear(c, carry):
        lead_of[c] = -1
        return carry

    lax.fori_loop(0, CBA, clear, 0, unroll=16)

    def note(r, carry):
        used, dups = carry
        for k in range(2):
            c = pattern[k + 1, r]
            s = 2 * r + k
            was = lead_of[c]
            new = (was < 0).astype(jnp.int32)
            lead = jnp.where(was < 0, s, was)
            lead_of[c] = lead
            head[s] = lead
            coupled[used] = c
            slot[used] = s
            dup_to[dups] = lead
            dup_from[dups] = s
            used, dups = used + new, dups + 1 - new
        return used, dups

    used, dups = lax.fori_loop(0, RB, note, (0, 0), unroll=4)

    def place(c, unused):
        free[unused] = c
        return unused + (lead_of[c] < 0).astype(jnp.int32)

    lax.fori_loop(0, CBA, place, 0, unroll=8)

    def fill(j, carry):
        coupled[j] = free[64 + j - used]
        slot[j] = ZERO_SLOT
        return carry

    lax.fori_loop(used, 64, fill, 0)
    if is_hub:
        mine = jnp.where(cyl == 0, counts_in[...], 0)
        counts[...] = down(mine + first_counts[...] + second_counts[...] + third_counts[...])
    else:
        counts[...] = down(counts_in[...])
    hot = one_hot(node_of[...])
    hot_low = hot.astype(jnp.bfloat16)[:, :NODES]
    hot_turned = hot.T[:NODES].astype(jnp.bfloat16)

    for one in (back, back_odd):
        one[:, cols(ZERO_SLOT)] = jnp.zeros((ROWS, BLK), jnp.float32)
    def arrange(r, carry):
        for k in range(3):
            tall[r, k * BLK : (k + 1) * BLK, :] = wide[r, :, k * BLK : (k + 1) * BLK].T
        return carry

    for n in range(4):
        for one in block_copies[n]:
            one.wait()
        lax.fori_loop(8 * n, 8 * n + 8, arrange, 0, unroll=8)
    for one in own_copies:
        one.wait()
    dual_copy.wait()

    def choose(live, new, old):
        return new if live is None else jnp.where(live, new, old)

    def spread(r, low, out, live):
        product = dot(low, wide[r])
        out[:, 2 * r * BLK : (2 * r + 2) * BLK] = product[:, BLK:]
        at = slice(r * BLK, (r + 1) * BLK)
        now = z_own[:, at]
        cost = gc[:, NNA + r * BLK : NNA + (r + 1) * BLK]
        fresh = jnp.clip(now + TAU * (product[:, :BLK] - cost), 0.0, 1.0)
        ext_own[:, at] = (fresh + fresh - now).astype(jnp.bfloat16)
        z_own[:, at] = choose(live, fresh, now)

    def merge(out):
        def step(k, carry):
            to = cols(dup_to[k])
            out[:, to] += out[:, cols(dup_from[k])]
            return carry

        lax.fori_loop(0, dups, step, 0)

    def loose(j, lives):
        c = cols(free[j])
        now = z[:, c]
        shift = d[:, c]
        for t in range(6):
            fresh = jnp.clip(now * inv + shift, 0.0, 1.0)
            now = fresh if t < 3 else jnp.where(lives[t - 3], fresh, now)
        z_free[:, cols(j)] = now

    def touch(before, after, back_in, live, lives, base, loose_count):
        for r in range(RB):
            for k in range(2):
                c = cols(coupled[2 * r + k])
                s = cols(slot[2 * r + k])
                now = before[:, c]
                fresh = jnp.clip(now * inv + back_in[:, s] * coef + d[:, c], 0.0, 1.0)
                ext[:, s] = (fresh + fresh - now).astype(jnp.bfloat16)
                after[:, c] = choose(live, fresh, now)
            if r < loose_count:
                loose(base + r, lives)

    def image(live):
        for r in range(RB):
            at = slice(r * BLK, (r + 1) * BLK)
            left = [ext_own[:, at], ext[:, cols(head[2 * r])], ext[:, cols(head[2 * r + 1])]]
            product = dot(jnp.concatenate(left, axis=1), tall[r])
            old = u[:, at]
            new = choose(live, jnp.maximum(0.0, old + SIGMA * (rh[:, at] - product)), old)
            u[:, at] = new
            uq[:, at] = new.astype(jnp.bfloat16)

    def turn(t, before, after, back_in, back_out, base, loose_count):
        live = counts[...] > t
        lives = [counts[...] > k for k in range(3, 6)]
        touch(before, after, back_in, live, lives, base, loose_count)
        image(live)
        next_live = counts[...] > t + 1
        for r in range(RB):
            spread(r, uq[:, r * BLK : (r + 1) * BLK], back_out, next_live)
        merge(back_out)

    def send(src, dst, k):
        one = pltpu.make_async_copy(src, dst, osem.at[k])
        one.start()
        return one

    def sum_nodes(block):
        high, low = split(z[:, cols(CB1 + block)])
        first = jnp.sum(z[:, cols(block)], axis=0, keepdims=True)
        return dot(hot_turned, high) + dot(hot_turned, low), first

    outs = []
    for r in range(RB):
        spread(r, u[:, r * BLK : (r + 1) * BLK].astype(jnp.bfloat16), back, None)
    merge(back)
    first_copy.wait()
    node_copy.wait()
    for n in range(NNA // CHUNK):
        for one in chunk_copies[n]:
            one.wait()

        def prepare(c, carry):
            if n * CHUNK < N1:
                target = jnp.broadcast_to(firsts[pl.ds(c, 1), :], (ROWS, BLK))
            else:
                high, low = split(nodes[:, cols(c - CB1)])
                target = dot(hot_low, high) + dot(hot_low, low)
            d[:, cols(c)] = pull * target - coef * (gc[:, cols(c)] + gm[:, cols(c)])
            return carry

        lax.fori_loop(n * PER, (n + 1) * PER, prepare, 0, unroll=8)
    rhs_copy.wait()

    def pair(i, carry):
        turn(2 * i, z, z_odd, back, back_odd, 16 * i, 16)
        turn(2 * i + 1, z_odd, z, back_odd, back, 0, 0)
        return carry

    lax.fori_loop(0, 2, pair, 0)
    turn(4, z, z_odd, back, back_odd, 32, 32)
    final = counts[...] > 5
    touch(z_odd, z, back_odd, final, None, 0, 0)

    def put_back(j, carry):
        z[:, cols(free[j])] = z_free[:, cols(j)]
        return carry

    lax.fori_loop(0, 64, put_back, 0, unroll=8)

    if is_hub:
        own_copy.wait()
        own = extra[0]

        def linear(c, acc):
            weight = gm[:, cols(c)] + rho * z[:, cols(c)]
            gm[:, cols(c)] = weight
            return acc + (gc[:, cols(c)] + weight) * own[:, cols(c)]

        def cost(c, acc):
            return acc + gc[:, cols(c)] * own[:, cols(c)]

        total = jnp.zeros((ROWS, BLK), jnp.float32)
        for n in range(NNA // CHUNK):
            total = lax.fori_loop(n * PER, (n + 1) * PER, linear, total, unroll=4)
            at = pl.ds(n * CHUNK, CHUNK)
            outs.append(send(gm.at[:, at], weights.at[:, at], n))
        total = lax.fori_loop(CBA, NZ // BLK, cost, total, unroll=4)
        lagrange[...] = jnp.sum(total.reshape(ROWS // 8, 8, BLK), axis=0)
    else:
        outs += [send(z, primal.at[0, :, pl.ds(0, NNA)], 0), send(z_own, primal.at[0, :, pl.ds(NNA, NZ - NNA)], 6)]
        tally = jnp.sum(hot, axis=0, keepdims=True)
        zeros = jnp.zeros((SHARD - HALF - 2, BLK), jnp.float32)

        image(final)
        outs.append(send(u, dual.at[0], 1))

        def shard(m, carry):
            for c in range(N_CYL):
                block = c * PER + m
                high, low = split(z[:, cols(CB1 + block)])
                node_sum = dot(hot_turned, high) + dot(hot_turned, low)
                first_sum = jnp.sum(z[:, cols(block)], axis=0, keepdims=True)
                tail = jnp.concatenate([first_sum, tally, zeros], axis=0)
                for half in range(2):
                    at = (2 * m + half) * N_CYL + c
                    extra[0][at, :HALF, :] = node_sum[half * HALF : (half + 1) * HALF]
                    extra[0][at, HALF:, :] = tail
            return carry

        for n in range(4):
            lax.fori_loop(4 * n, 4 * n + 4, shard, 0, unroll=4)
            at = pl.ds(GROUPS * n, GROUPS)
            outs.append(send(extra[0].at[at], sums.at[at], 2 + n))
    for one in outs:
        one.wait()


def solve(kind, *args):
    f32, bf16, i32 = jnp.float32, jnp.bfloat16, jnp.int32
    V = pltpu.VMEM
    wide, tall = (RB, BLK, 3 * BLK), (RB, 3 * BLK, BLK)
    shares = (GROUPS * N_CYL, SHARD, BLK)
    if kind == "hub":
        outs = [((ROWS, NNA), f32), ((8, BLK), f32)]
        extra, out_specs, in_more = [V((ROWS, NZ), f32)], [HBM, VM], [HBM, HBM] + [VM] * 3
    else:
        outs = [((1, ROWS, NZ), f32), ((1, ROWS, M), f32), (shares, f32)]
        extra, out_specs, in_more = [V(shares, f32)], [HBM] * 3, [HBM]
    return pl.pallas_call(
        functools.partial(solve_kernel, kind),
        out_shape=[jax.ShapeDtypeStruct(*one) for one in outs],
        in_specs=[SM, SM, VM, VM] + [HBM] * 7 + in_more,
        out_specs=out_specs,
        scratch_shapes=[
            *[pltpu.SMEM((136,), i32)] * 7,
            V((ROWS, BLK), i32),
            V((ROWS, NNA), f32),
            V((ROWS, NNA), f32),
            V((ROWS, M), f32),
            V((ROWS, 64 * BLK), f32),
            V((ROWS, NNA), f32),
            V((ROWS, NZ), f32),
            V((ROWS, NNA), f32),
            V((ROWS, 65 * BLK), f32),
            V((ROWS, 65 * BLK), f32),
            V((ROWS, 65 * BLK), bf16),
            V((ROWS, M), bf16),
            V((ROWS, M), f32),
            V((ROWS, M), bf16),
            V((ROWS, M), f32),
            V(wide, bf16),
            V(tall, bf16),
            V((NODES, N2), f32),
            V((CB1, BLK), f32),
            *extra,
            pltpu.SemaphoreType.DMA((56,)),
            pltpu.SemaphoreType.DMA((8,)),
        ],
        compiler_params=pltpu.CompilerParams(vmem_limit_bytes=VMEM_LIMIT),
        cost_estimate=pl.CostEstimate(flops=10**10, bytes_accessed=4 * 10**7, transcendentals=0),
        name="solve_" + kind,
    )(*args)


def average_kernel(prox, sums, lagrange, out):
    cyl = lax.axis_index("cyl")
    half = lax.axis_index("scen") % 2
    totals = [sums[c] for c in range(N_CYL)]
    for i in range(1, GROUPS):
        totals = [total + sums[i * N_CYL + c] for c, total in enumerate(totals)]
    hub = totals[0]
    tally = jnp.broadcast_to(hub[HALF + 1 : HALF + 2], (HALF, BLK))
    lanes = lax.broadcasted_iota(jnp.int32, (HALF, BLK), 1)
    wanted = lax.broadcasted_iota(jnp.int32, (HALF, BLK), 0) + half * HALF
    count = jnp.sum(jnp.where(lanes == wanted, tally, 0.0), axis=1, keepdims=True)
    low = hub[:HALF] / count
    first = hub[HALF : HALF + 1] * (1.0 / SCEN)
    once = jnp.where(half == 0, first, jnp.zeros_like(first))
    lane = lax.broadcasted_iota(jnp.int32, (1, BLK), 1)
    scalars = jnp.where(lane == cyl, jnp.sum(lagrange[...]), 0.0)
    for c, total in enumerate(totals):
        both = jnp.sum(low * total[:HALF]) + jnp.sum(once * total[HALF : HALF + 1])
        scalars = scalars - jnp.where(lane == c, prox[0] * both, 0.0)
    top = low[: SHARD // 2]
    zeros = jnp.zeros((SHARD - HALF - 2, BLK), jnp.float32)
    bottom = jnp.concatenate([low[SHARD // 2 :], first, scalars, zeros], axis=0)

    def put(i, carry):
        for c in range(N_CYL):
            out[i * N_CYL + c] = bottom if c % 2 else top
        return carry

    lax.fori_loop(0, GROUPS, put, 0, unroll=2)


def average(prox, sums, lagrange):
    return pl.pallas_call(
        average_kernel,
        out_shape=jax.ShapeDtypeStruct((GROUPS * N_CYL, SHARD // 2, BLK), jnp.float32),
        in_specs=[SM, VM, VM],
        out_specs=VM,
        cost_estimate=pl.CostEstimate(flops=10**7, bytes_accessed=4 * 10**6, transcendentals=0),
        name="average",
    )(prox, sums, lagrange)


def fetch_shards(mine, other, shards, sem):
    core = lax.axis_index("cyl") % 2
    parts = [
        pltpu.make_async_copy(mine, shards.at[core], sem.at[0]),
        pltpu.make_async_copy(other, shards.at[1 - core], sem.at[1]),
    ]
    for one in parts:
        one.start()
    return parts


def averages(shards, c, m):
    lead = 2 * N_CYL * m + c
    rest = slice(0, HALF - SHARD // 2)
    pieces = [shards[0, lead], shards[1, lead, rest, :], shards[0, lead + N_CYL], shards[1, lead + N_CYL, rest, :]]
    return jnp.concatenate(pieces, axis=0), shards[1, lead, pl.ds(HALF - SHARD // 2, 1), :]


def update_kernel(
    prox, mine, other, weights, node_of, multipliers, first_out, node_out, objectives, shards, w, nodes, sem, osem
):
    rho = prox[0]
    parts = fetch_shards(mine, other, shards, sem)
    chunks = []
    for n in range(NNA // CHUNK):
        at = pl.ds(n * CHUNK, CHUNK)
        chunks.append(pltpu.make_async_copy(weights.at[:, at], w.at[:, at], sem.at[2 + n]))
        chunks[-1].start()
    hot = one_hot(node_of[...]).astype(jnp.bfloat16)[:, :NODES]
    for one in parts:
        one.wait()
    outs = []
    for n in range(NNA // CHUNK):
        chunks[n].wait()

        def step(m, carry):
            node_avg, first = averages(shards, n % N_CYL, m)
            block = (n % N_CYL) * PER + m
            if n * CHUNK < N1:
                first_out[pl.ds(block, 1), :] = first
                own = jnp.broadcast_to(first, (ROWS, BLK))
            else:
                nodes[:, cols(block)] = node_avg
                high, low = split(node_avg)
                own = dot(hot, high) + dot(hot, low)
            c = cols(n * PER + m)
            w[:, c] = w[:, c] - rho * own
            return carry

        lax.fori_loop(0, PER, step, 0, unroll=8)
        at = pl.ds(n * CHUNK, CHUNK)
        outs.append(pltpu.make_async_copy(w.at[:, at], multipliers.at[:, at], osem.at[n]))
        outs[-1].start()
        if n * CHUNK >= N1:
            at = pl.ds(n * CHUNK - N1, CHUNK)
            outs.append(pltpu.make_async_copy(nodes.at[:, at], node_out.at[:, at], osem.at[n + 4]))
            outs[-1].start()

    def add(i, acc):
        return acc + shards[1, i, 8:, :]

    total = lax.fori_loop(1, GROUPS * N_CYL, add, shards[1, 0, 8:, :], unroll=8)
    lane = lax.broadcasted_iota(jnp.int32, (1, BLK), 1)
    for c in range(N_CYL):
        objectives[c] = jnp.sum(jnp.where(lane == c, total[1:2], 0.0)) * (1.0 / SCEN)
    for one in outs:
        one.wait()


def update(prox, mine, other, weights, node_of):
    f32 = jnp.float32
    V = pltpu.VMEM
    return pl.pallas_call(
        update_kernel,
        out_shape=[
            jax.ShapeDtypeStruct((ROWS, NNA), f32),
            jax.ShapeDtypeStruct((CB1, BLK), f32),
            jax.ShapeDtypeStruct((NODES, N2), f32),
            jax.ShapeDtypeStruct((N_CYL,), f32),
        ],
        in_specs=[SM, ANY, ANY, HBM, VM],
        out_specs=[HBM, VM, HBM, SM],
        scratch_shapes=[
            V((2, GROUPS * N_CYL, SHARD // 2, BLK), f32),
            V((ROWS, NNA), f32),
            V((NODES, N2), f32),
            pltpu.SemaphoreType.DMA((12,)),
            pltpu.SemaphoreType.DMA((12,)),
        ],
        compiler_params=pltpu.CompilerParams(vmem_limit_bytes=VMEM_LIMIT),
        cost_estimate=pl.CostEstimate(flops=10**9, bytes_accessed=2 * 10**7, transcendentals=0),
        name="update",
    )(prox, mine, other, weights, node_of)


def body(
    costs,
    rhs,
    multipliers,
    xbar_first_in,
    xbar_node_in,
    prox_weights,
    start_primal,
    start_dual,
    recourse_blocks,
    block_pattern,
    node_of,
    pdhg_counts,
):
    hub_counts = [lax.ppermute(pdhg_counts, "cyl", [(0, c)]) for c in range(1, N_CYL)]
    pattern = block_pattern.T
    node_row = node_of.reshape(1, ROWS)
    data = (costs, rhs, multipliers, xbar_first_in.reshape(CB1, BLK), xbar_node_in, start_primal, start_dual)
    ints = (pattern, prox_weights, node_row, pdhg_counts)
    primal, dual, sums = solve("own", *ints, *data, recourse_blocks)
    sums, *hub_counts = lax.optimization_barrier((sums, *hub_counts))
    gathered = lax.all_to_all(sums, ALL, 0, 0, tiled=True)
    weights, lagrange = solve("hub", *ints, *data, recourse_blocks, primal, *hub_counts)
    shares = average(prox_weights, gathered, lagrange)
    mine = lax.all_to_all(shares, ALL, 0, 0, tiled=True)
    other = lax.ppermute(mine, "cyl", [(0, 1), (1, 0), (2, 3), (3, 2)])
    new_multipliers, first, xbar_node, objectives = update(prox_weights, mine, other, weights, node_row)
    return (primal, dual, first.reshape(N1), xbar_node, new_multipliers, objectives)


def solution(mesh):
    return jax.shard_map(
        body,
        mesh=mesh,
        in_specs=(
            P("scen", None),
            P("scen", None),
            P("scen", None),
            P(),
            P(),
            P(),
            P("scen", None),
            P("scen", None),
            P(),
            P(),
            P("scen"),
            P("cyl", "scen"),
        ),
        out_specs=(P("cyl", "scen", None), P("cyl", "scen", None), P(), P(), P("scen", None), P()),
        check_vma=False,
    )
```

```python
import functools

import jax
import jax.numpy as jnp
from jax import lax
from jax.experimental import pallas as pl
from jax.experimental.pallas import tpu as pltpu
from jax.sharding import PartitionSpec as P

N1 = 8192
N2 = 8192
NNA = 16384
M = 4096
NZ = 20480
BLK = 128
RB = 32
Q = 96
NODES = 48
SCEN = 2048
ROWS = 64
N_CYL = 4
GROUPS = 32
HALF = 24
SHARD = 32
CB1 = N1 // BLK
CBA = NNA // BLK
CHUNK = 2048
PER = CHUNK // BLK
ZERO_SLOT = 64
VMEM_LIMIT = 62 * 2**20
ALL = ("scen", "cyl")

TAU = 0.4
SIGMA = 0.4

ANY = pl.BlockSpec(memory_space=pl.ANY)
HBM = pl.BlockSpec(memory_space=pltpu.HBM)
VM = pl.BlockSpec(memory_space=pltpu.VMEM)
SM = pl.BlockSpec(memory_space=pltpu.SMEM)


def cols(c):
    return pl.ds(pl.multiple_of(c * BLK, BLK), BLK)


def split(value):
    high = value.astype(jnp.bfloat16)
    return high, (value - high.astype(jnp.float32)).astype(jnp.bfloat16)


def dot(a, b):
    return jnp.dot(a, b, preferred_element_type=jnp.float32)


def down(row):
    row = jnp.broadcast_to(row, (ROWS, ROWS))
    here = lax.broadcasted_iota(jnp.int32, (ROWS, ROWS), 0) == lax.broadcasted_iota(jnp.int32, (ROWS, ROWS), 1)
    return jnp.broadcast_to(jnp.sum(jnp.where(here, row, 0), axis=1, keepdims=True), (ROWS, BLK))


def one_hot(node_row):
    lanes = lax.broadcasted_iota(jnp.int32, (ROWS, BLK), 1)
    return (down(node_row) == lanes).astype(jnp.float32)


def solve_kernel(kind, *refs):
    (pattern, prox, node_of, counts_in, costs, rhs, mult, first_in, node_in, start, start_dual) = refs[:11]
    refs = refs[11:]
    is_hub = kind == "hub"
    if is_hub:
        (blocks, own_in, weights, lagrange) = refs[:4]
        refs = refs[4:]
    else:
        blocks, primal, dual, sums = refs[:4]
        refs = refs[4:]
    (
        head, lead_of, coupled, slot, free, dup_to, dup_from,
        counts, z, z_odd, z_own, z_free, d, gc, gm, back, back_odd, ext, ext_own, u, uq, rh, wide, tall, nodes, firsts,
        extra, sem, osem,
    ) = (*refs[:26], refs[26:-2], *refs[-2:])
    extra, small, head_smem = extra[:-3], extra[-3:-1], extra[-1]
    pattern_copy = pltpu.make_async_copy(pattern, head_smem, sem.at[52])
    small_copies = [
        pltpu.make_async_copy(node_of, small[0], sem.at[53]),
        pltpu.make_async_copy(counts_in.at[pl.ds(0, 1)], small[1], sem.at[54]),
    ]
    for one in [pattern_copy, *small_copies]:
        one.start()
    pattern = head_smem
    cyl = lax.axis_index("cyl")
    rho = prox[0] if is_hub else prox[cyl]
    inv = jnp.broadcast_to((1.0 / (1.0 + TAU * jnp.full((8, BLK), rho, jnp.float32)))[:1], (ROWS, BLK))
    coef = TAU * inv
    pull = TAU * rho * inv

    def copy(src, dst, k):
        return pltpu.make_async_copy(src, dst, sem.at[k])

    block_copies = []
    for n in range(4):
        at = pl.ds(8 * n, 8)
        group = [copy(blocks.at[at, k], wide.at[at, :, pl.ds(k * BLK, BLK)], 40 + 3 * n + k) for k in range(3)]
        block_copies.append(group)
    dual_copy = copy(start_dual, u, 2)
    node_copy = copy(node_in, nodes, 3)
    first_copy = copy(first_in, firsts, 4)
    rhs_copy = copy(rhs, rh, 5)
    chunk_copies = []
    for n in range(NZ // CHUNK):
        at = pl.ds(n * CHUNK, CHUNK)
        where = z.at[:, at] if n * CHUNK < NNA else z_own.at[:, pl.ds(n * CHUNK - NNA, CHUNK)]
        group = [copy(costs.at[:, at], gc.at[:, at], 6 + 3 * n), copy(start.at[:, at], where, 7 + 3 * n)]
        if n * CHUNK < NNA:
            group.append(copy(mult.at[:, at], gm.at[:, at], 8 + 3 * n))
        chunk_copies.append(group)
    own_copies = sum(chunk_copies[NNA // CHUNK :], [])
    for one in [*sum(block_copies, []), dual_copy, *own_copies, first_copy]:
        one.start()
    for n, group in enumerate(chunk_copies[: NNA // CHUNK]):
        if n == N1 // CHUNK - 1:
            node_copy.start()
        for one in group:
            one.start()
    rhs_copy.start()
    if is_hub:
        own_copy = copy(own_in.at[0], extra[0], 0)
        own_copy.start()

    pattern_copy.wait()

    def clear(c, carry):
        lead_of[c] = -1
        return carry

    lax.fori_loop(0, CBA, clear, 0, unroll=16)

    def note(r, carry):
        used, dups = carry
        for k in range(2):
            c = pattern[k + 1, r]
            s = 2 * r + k
            was = lead_of[c]
            new = (was < 0).astype(jnp.int32)
            lead = jnp.where(was < 0, s, was)
            lead_of[c] = lead
            head[s] = lead
            coupled[used] = c
            slot[used] = s
            dup_to[dups] = lead
            dup_from[dups] = s
            used, dups = used + new, dups + 1 - new
        return used, dups

    used, dups = lax.fori_loop(0, RB, note, (0, 0), unroll=4)

    def place(c, unused):
        free[unused] = c
        return unused + (lead_of[c] < 0).astype(jnp.int32)

    lax.fori_loop(0, CBA, place, 0, unroll=8)

    def fill(j, carry):
        coupled[j] = free[64 + j - used]
        slot[j] = ZERO_SLOT
        return carry

    lax.fori_loop(used, 64, fill, 0)
    for one in small_copies:
        one.wait()
    counts[...] = down(small[1][...].reshape(1, ROWS))
    hot = one_hot(small[0][...])
    hot_low = hot.astype(jnp.bfloat16)[:, :NODES]
    hot_turned = hot.T[:NODES].astype(jnp.bfloat16)

    for one in (back, back_odd):
        one[:, cols(ZERO_SLOT)] = jnp.zeros((ROWS, BLK), jnp.float32)
    def arrange(r, carry):
        for k in range(3):
            tall[r, k * BLK : (k + 1) * BLK, :] = wide[r, :, k * BLK : (k + 1) * BLK].T
        return carry

    for n in range(4):
        for one in block_copies[n]:
            one.wait()
        lax.fori_loop(8 * n, 8 * n + 8, arrange, 0, unroll=8)
    for one in own_copies:
        one.wait()
    dual_copy.wait()

    def choose(live, new, old):
        return new if live is None else jnp.where(live, new, old)

    def spread(r, low, out, live):
        product = dot(low, wide[r])
        out[:, 2 * r * BLK : (2 * r + 2) * BLK] = product[:, BLK:]
        at = slice(r * BLK, (r + 1) * BLK)
        now = z_own[:, at]
        cost = gc[:, NNA + r * BLK : NNA + (r + 1) * BLK]
        fresh = jnp.clip(now + TAU * (product[:, :BLK] - cost), 0.0, 1.0)
        ext_own[:, at] = (fresh + fresh - now).astype(jnp.bfloat16)
        z_own[:, at] = choose(live, fresh, now)

    def merge(out):
        def step(k, carry):
            to = cols(dup_to[k])
            out[:, to] += out[:, cols(dup_from[k])]
            return carry

        lax.fori_loop(0, dups, step, 0)

    def loose(j, lives):
        c = cols(free[j])
        now = z[:, c]
        shift = d[:, c]
        for t in range(6):
            fresh = jnp.clip(now * inv + shift, 0.0, 1.0)
            now = fresh if t < 3 else jnp.where(lives[t - 3], fresh, now)
        z_free[:, cols(j)] = now

    def touch(before, after, back_in, live, lives, base, loose_count):
        for r in range(RB):
            for k in range(2):
                c = cols(coupled[2 * r + k])
                s = cols(slot[2 * r + k])
                now = before[:, c]
                fresh = jnp.clip(now * inv + back_in[:, s] * coef + d[:, c], 0.0, 1.0)
                ext[:, s] = (fresh + fresh - now).astype(jnp.bfloat16)
                after[:, c] = choose(live, fresh, now)
            if r < loose_count:
                loose(base + r, lives)

    def image(live):
        for r in range(RB):
            at = slice(r * BLK, (r + 1) * BLK)
            left = [ext_own[:, at], ext[:, cols(head[2 * r])], ext[:, cols(head[2 * r + 1])]]
            product = dot(jnp.concatenate(left, axis=1), tall[r])
            old = u[:, at]
            new = choose(live, jnp.maximum(0.0, old + SIGMA * (rh[:, at] - product)), old)
            u[:, at] = new
            uq[:, at] = new.astype(jnp.bfloat16)

    def turn(t, before, after, back_in, back_out, base, loose_count):
        live = counts[...] > t
        lives = [counts[...] > k for k in range(3, 6)]
        touch(before, after, back_in, live, lives, base, loose_count)
        image(live)
        next_live = counts[...] > t + 1
        for r in range(RB):
            spread(r, uq[:, r * BLK : (r + 1) * BLK], back_out, next_live)
        merge(back_out)

    def send(src, dst, k):
        one = pltpu.make_async_copy(src, dst, osem.at[k])
        one.start()
        return one

    def sum_nodes(block):
        high, low = split(z[:, cols(CB1 + block)])
        first = jnp.sum(z[:, cols(block)], axis=0, keepdims=True)
        return dot(hot_turned, high) + dot(hot_turned, low), first

    outs = []
    for r in range(RB):
        spread(r, u[:, r * BLK : (r + 1) * BLK].astype(jnp.bfloat16), back, None)
    merge(back)
    first_copy.wait()
    node_copy.wait()
    for n in range(NNA // CHUNK):
        for one in chunk_copies[n]:
            one.wait()

        def prepare(c, carry):
            if n * CHUNK < N1:
                target = jnp.broadcast_to(firsts[pl.ds(c, 1), :], (ROWS, BLK))
            else:
                high, low = split(nodes[:, cols(c - CB1)])
                target = dot(hot_low, high) + dot(hot_low, low)
            d[:, cols(c)] = pull * target - coef * (gc[:, cols(c)] + gm[:, cols(c)])
            return carry

        lax.fori_loop(n * PER, (n + 1) * PER, prepare, 0, unroll=8)
    rhs_copy.wait()

    def pair(i, carry):
        turn(2 * i, z, z_odd, back, back_odd, 16 * i, 16)
        turn(2 * i + 1, z_odd, z, back_odd, back, 0, 0)
        return carry

    lax.fori_loop(0, 2, pair, 0)
    turn(4, z, z_odd, back, back_odd, 32, 32)
    final = counts[...] > 5
    touch(z_odd, z, back_odd, final, None, 0, 0)

    def put_back(j, carry):
        z[:, cols(free[j])] = z_free[:, cols(j)]
        return carry

    lax.fori_loop(0, 64, put_back, 0, unroll=8)

    if is_hub:
        own_copy.wait()
        own = extra[0]

        def linear(c, acc):
            weight = gm[:, cols(c)] + rho * z[:, cols(c)]
            gm[:, cols(c)] = weight
            return acc + (gc[:, cols(c)] + weight) * own[:, cols(c)]

        def cost(c, acc):
            return acc + gc[:, cols(c)] * own[:, cols(c)]

        total = jnp.zeros((ROWS, BLK), jnp.float32)
        for n in range(NNA // CHUNK):
            total = lax.fori_loop(n * PER, (n + 1) * PER, linear, total, unroll=4)
            at = pl.ds(n * CHUNK, CHUNK)
            outs.append(send(gm.at[:, at], weights.at[:, at], n))
        total = lax.fori_loop(CBA, NZ // BLK, cost, total, unroll=4)
        lagrange[...] = jnp.sum(total.reshape(ROWS // 8, 8, BLK), axis=0)
    else:
        outs += [send(z, primal.at[0, :, pl.ds(0, NNA)], 0), send(z_own, primal.at[0, :, pl.ds(NNA, NZ - NNA)], 6)]
        tally = jnp.sum(hot, axis=0, keepdims=True)
        zeros = jnp.zeros((SHARD - HALF - 2, BLK), jnp.float32)

        image(final)
        outs.append(send(u, dual.at[0], 1))

        def shard(m, carry):
            for c in range(N_CYL):
                block = c * PER + m
                high, low = split(z[:, cols(CB1 + block)])
                node_sum = dot(hot_turned, high) + dot(hot_turned, low)
                first_sum = jnp.sum(z[:, cols(block)], axis=0, keepdims=True)
                tail = jnp.concatenate([first_sum, tally, zeros], axis=0)
                for half in range(2):
                    at = (2 * m + half) * N_CYL + c
                    extra[0][at, :HALF, :] = node_sum[half * HALF : (half + 1) * HALF]
                    extra[0][at, HALF:, :] = tail
            return carry

        for n in range(4):
            lax.fori_loop(4 * n, 4 * n + 4, shard, 0, unroll=4)
            at = pl.ds(GROUPS * n, GROUPS)
            outs.append(send(extra[0].at[at], sums.at[at], 2 + n))
    for one in outs:
        one.wait()


def solve(kind, *args):
    f32, bf16, i32 = jnp.float32, jnp.bfloat16, jnp.int32
    V = pltpu.VMEM
    wide, tall = (RB, BLK, 3 * BLK), (RB, 3 * BLK, BLK)
    shares = (GROUPS * N_CYL, SHARD, BLK)
    if kind == "hub":
        outs = [((ROWS, NNA), f32), ((8, BLK), f32)]
        extra, out_specs, in_more = [V((ROWS, NZ), f32)], [HBM, VM], [HBM, HBM]
    else:
        outs = [((1, ROWS, NZ), f32), ((1, ROWS, M), f32), (shares, f32)]
        extra, out_specs, in_more = [V(shares, f32)], [HBM] * 3, [HBM]
    return pl.pallas_call(
        functools.partial(solve_kernel, kind),
        out_shape=[jax.ShapeDtypeStruct(*one) for one in outs],
        in_specs=[HBM, SM, HBM, HBM] + [HBM] * 7 + in_more,
        out_specs=out_specs,
        scratch_shapes=[
            *[pltpu.SMEM((136,), i32)] * 7,
            V((ROWS, BLK), i32),
            V((ROWS, NNA), f32),
            V((ROWS, NNA), f32),
            V((ROWS, M), f32),
            V((ROWS, 64 * BLK), f32),
            V((ROWS, NNA), f32),
            V((ROWS, NZ), f32),
            V((ROWS, NNA), f32),
            V((ROWS, 65 * BLK), f32),
            V((ROWS, 65 * BLK), f32),
            V((ROWS, 65 * BLK), bf16),
            V((ROWS, M), bf16),
            V((ROWS, M), f32),
            V((ROWS, M), bf16),
            V((ROWS, M), f32),
            V(wide, bf16),
            V(tall, bf16),
            V((NODES, N2), f32),
            V((CB1, BLK), f32),
            *extra,
            V((1, ROWS), i32),
            V((1, 1, ROWS), i32),
            pltpu.SMEM((3, RB), i32),
            pltpu.SemaphoreType.DMA((60,)),
            pltpu.SemaphoreType.DMA((8,)),
        ],
        compiler_params=pltpu.CompilerParams(vmem_limit_bytes=VMEM_LIMIT),
        cost_estimate=pl.CostEstimate(flops=10**10, bytes_accessed=4 * 10**7, transcendentals=0),
        name="solve_" + kind,
    )(*args)


def average_kernel(prox, sums, lagrange, out):
    cyl = lax.axis_index("cyl")
    half = lax.axis_index("scen") % 2
    totals = [sums[c] for c in range(N_CYL)]
    for i in range(1, GROUPS):
        totals = [total + sums[i * N_CYL + c] for c, total in enumerate(totals)]
    hub = totals[0]
    tally = jnp.broadcast_to(hub[HALF + 1 : HALF + 2], (HALF, BLK))
    lanes = lax.broadcasted_iota(jnp.int32, (HALF, BLK), 1)
    wanted = lax.broadcasted_iota(jnp.int32, (HALF, BLK), 0) + half * HALF
    count = jnp.sum(jnp.where(lanes == wanted, tally, 0.0), axis=1, keepdims=True)
    low = hub[:HALF] / count
    first = hub[HALF : HALF + 1] * (1.0 / SCEN)
    once = jnp.where(half == 0, first, jnp.zeros_like(first))
    lane = lax.broadcasted_iota(jnp.int32, (1, BLK), 1)
    scalars = jnp.where(lane == cyl, jnp.sum(lagrange[...]), 0.0)
    for c, total in enumerate(totals):
        both = jnp.sum(low * total[:HALF]) + jnp.sum(once * total[HALF : HALF + 1])
        scalars = scalars - jnp.where(lane == c, prox[0] * both, 0.0)
    top = low[: SHARD // 2]
    zeros = jnp.zeros((SHARD - HALF - 2, BLK), jnp.float32)
    bottom = jnp.concatenate([low[SHARD // 2 :], first, scalars, zeros], axis=0)

    def put(i, carry):
        for c in range(N_CYL):
            out[i * N_CYL + c] = bottom if c % 2 else top
        return carry

    lax.fori_loop(0, GROUPS, put, 0, unroll=2)


def average(prox, sums, lagrange):
    return pl.pallas_call(
        average_kernel,
        out_shape=jax.ShapeDtypeStruct((GROUPS * N_CYL, SHARD // 2, BLK), jnp.float32),
        in_specs=[SM, VM, VM],
        out_specs=VM,
        cost_estimate=pl.CostEstimate(flops=10**7, bytes_accessed=4 * 10**6, transcendentals=0),
        name="average",
    )(prox, sums, lagrange)


def fetch_shards(mine, other, shards, sem):
    core = lax.axis_index("cyl") % 2
    parts = [
        pltpu.make_async_copy(mine, shards.at[core], sem.at[0]),
        pltpu.make_async_copy(other, shards.at[1 - core], sem.at[1]),
    ]
    for one in parts:
        one.start()
    return parts


def averages(shards, c, m):
    lead = 2 * N_CYL * m + c
    rest = slice(0, HALF - SHARD // 2)
    pieces = [shards[0, lead], shards[1, lead, rest, :], shards[0, lead + N_CYL], shards[1, lead + N_CYL, rest, :]]
    return jnp.concatenate(pieces, axis=0), shards[1, lead, pl.ds(HALF - SHARD // 2, 1), :]


def update_kernel(
    prox, mine, other, weights, node_of, multipliers, first_out, node_out, objectives, shards, w, nodes, sem, osem
):
    rho = prox[0]
    parts = fetch_shards(mine, other, shards, sem)
    chunks = []
    for n in range(NNA // CHUNK):
        at = pl.ds(n * CHUNK, CHUNK)
        chunks.append(pltpu.make_async_copy(weights.at[:, at], w.at[:, at], sem.at[2 + n]))
        chunks[-1].start()
    hot = one_hot(node_of[...]).astype(jnp.bfloat16)[:, :NODES]
    for one in parts:
        one.wait()
    outs = []
    for n in range(NNA // CHUNK):
        chunks[n].wait()

        def step(m, carry):
            node_avg, first = averages(shards, n % N_CYL, m)
            block = (n % N_CYL) * PER + m
            if n * CHUNK < N1:
                first_out[pl.ds(block, 1), :] = first
                own = jnp.broadcast_to(first, (ROWS, BLK))
            else:
                nodes[:, cols(block)] = node_avg
                high, low = split(node_avg)
                own = dot(hot, high) + dot(hot, low)
            c = cols(n * PER + m)
            w[:, c] = w[:, c] - rho * own
            return carry

        lax.fori_loop(0, PER, step, 0, unroll=8)
        at = pl.ds(n * CHUNK, CHUNK)
        outs.append(pltpu.make_async_copy(w.at[:, at], multipliers.at[:, at], osem.at[n]))
        outs[-1].start()
        if n * CHUNK >= N1:
            at = pl.ds(n * CHUNK - N1, CHUNK)
            outs.append(pltpu.make_async_copy(nodes.at[:, at], node_out.at[:, at], osem.at[n + 4]))
            outs[-1].start()

    def add(i, acc):
        return acc + shards[1, i, 8:, :]

    total = lax.fori_loop(1, GROUPS * N_CYL, add, shards[1, 0, 8:, :], unroll=8)
    lane = lax.broadcasted_iota(jnp.int32, (1, BLK), 1)
    for c in range(N_CYL):
        objectives[c] = jnp.sum(jnp.where(lane == c, total[1:2], 0.0)) * (1.0 / SCEN)
    for one in outs:
        one.wait()


def update(prox, mine, other, weights, node_of):
    f32 = jnp.float32
    V = pltpu.VMEM
    return pl.pallas_call(
        update_kernel,
        out_shape=[
            jax.ShapeDtypeStruct((ROWS, NNA), f32),
            jax.ShapeDtypeStruct((CB1, BLK), f32),
            jax.ShapeDtypeStruct((NODES, N2), f32),
            jax.ShapeDtypeStruct((N_CYL,), f32),
        ],
        in_specs=[SM, ANY, ANY, HBM, VM],
        out_specs=[HBM, VM, HBM, SM],
        scratch_shapes=[
            V((2, GROUPS * N_CYL, SHARD // 2, BLK), f32),
            V((ROWS, NNA), f32),
            V((NODES, N2), f32),
            pltpu.SemaphoreType.DMA((12,)),
            pltpu.SemaphoreType.DMA((12,)),
        ],
        compiler_params=pltpu.CompilerParams(vmem_limit_bytes=32 * 2**20),
        cost_estimate=pl.CostEstimate(flops=10**9, bytes_accessed=2 * 10**7, transcendentals=0),
        name="update",
    )(prox, mine, other, weights, node_of)


def body(
    costs,
    rhs,
    multipliers,
    xbar_first_in,
    xbar_node_in,
    prox_weights,
    start_primal,
    start_dual,
    recourse_blocks,
    block_pattern,
    node_of,
    pdhg_counts,
):
    own_counts = pdhg_counts.reshape(1, 1, ROWS)
    all_counts = lax.all_to_all(jnp.broadcast_to(own_counts, (N_CYL, 1, ROWS)), "cyl", 0, 0, tiled=True)
    pattern = block_pattern.T
    node_row = node_of.reshape(1, ROWS)
    data = (costs, rhs, multipliers, xbar_first_in.reshape(CB1, BLK), xbar_node_in, start_primal, start_dual)
    ints = (pattern, prox_weights, node_row)
    primal, dual, sums = solve("own", *ints, own_counts, *data, recourse_blocks)
    sums, all_counts = lax.optimization_barrier((sums, all_counts))
    gathered = lax.all_to_all(sums, ALL, 0, 0, tiled=True)
    weights, lagrange = solve("hub", *ints, all_counts, *data, recourse_blocks, primal)
    shares = average(prox_weights, gathered, lagrange)
    mine = lax.all_to_all(shares, ALL, 0, 0, tiled=True)
    other = lax.ppermute(mine, "cyl", [(0, 1), (1, 0), (2, 3), (3, 2)])
    new_multipliers, first, xbar_node, objectives = update(prox_weights, mine, other, weights, node_row)
    return (primal, dual, first.reshape(N1), xbar_node, new_multipliers, objectives)


def solution(mesh):
    return jax.shard_map(
        body,
        mesh=mesh,
        in_specs=(
            P("scen", None),
            P("scen", None),
            P("scen", None),
            P(),
            P(),
            P(),
            P("scen", None),
            P("scen", None),
            P(),
            P(),
            P("scen"),
            P("cyl", "scen"),
        ),
        out_specs=(P("cyl", "scen", None), P("cyl", "scen", None), P(), P(), P("scen", None), P()),
        check_vma=False,
    )
```

```python
import functools

import jax
import jax.numpy as jnp
from jax import lax
from jax.experimental import pallas as pl
from jax.experimental.pallas import tpu as pltpu
from jax.sharding import PartitionSpec as P

N1 = 8192
N2 = 8192
NNA = 16384
M = 4096
NZ = 20480
BLK = 128
RB = 32
Q = 96
NODES = 48
SCEN = 2048
ROWS = 64
N_CYL = 4
GROUPS = 32
HALF = 24
SHARD = 32
CB1 = N1 // BLK
CBA = NNA // BLK
CHUNK = 2048
PER = CHUNK // BLK
ZERO_SLOT = 64
VMEM_LIMIT = 62 * 2**20
ALL = ("scen", "cyl")

TAU = 0.4
SIGMA = 0.4

ANY = pl.BlockSpec(memory_space=pl.ANY)
HBM = pl.BlockSpec(memory_space=pltpu.HBM)
VM = pl.BlockSpec(memory_space=pltpu.VMEM)
SM = pl.BlockSpec(memory_space=pltpu.SMEM)


def cols(c):
    return pl.ds(pl.multiple_of(c * BLK, BLK), BLK)


def split(value):
    high = value.astype(jnp.bfloat16)
    return high, (value - high.astype(jnp.float32)).astype(jnp.bfloat16)


def dot(a, b):
    return jnp.dot(a, b, preferred_element_type=jnp.float32)


def down(row):
    row = jnp.broadcast_to(row, (ROWS, ROWS))
    here = lax.broadcasted_iota(jnp.int32, (ROWS, ROWS), 0) == lax.broadcasted_iota(jnp.int32, (ROWS, ROWS), 1)
    return jnp.broadcast_to(jnp.sum(jnp.where(here, row, 0), axis=1, keepdims=True), (ROWS, BLK))


def one_hot(node_row):
    lanes = lax.broadcasted_iota(jnp.int32, (ROWS, BLK), 1)
    return (down(node_row) == lanes).astype(jnp.float32)


def solve_kernel(kind, *refs):
    (pattern, prox, node_of, counts_in, costs, rhs, mult, first_in, node_in, start, start_dual) = refs[:11]
    refs = refs[11:]
    is_hub = kind == "hub"
    if is_hub:
        (blocks, own_in, weights, lagrange) = refs[:4]
        refs = refs[4:]
    else:
        blocks, primal, dual, sums = refs[:4]
        refs = refs[4:]
    (
        head, lead_of, coupled, slot, free, dup_to, dup_from,
        counts, z, z_odd, z_own, z_free, d, gc, gm, back, back_odd, ext, ext_own, u, uq, rh, wide, tall, nodes, firsts,
        extra, sem, osem,
    ) = (*refs[:26], refs[26:-2], *refs[-2:])
    extra, small, head_smem = extra[:-3], extra[-3:-1], extra[-1]
    pattern_copy = pltpu.make_async_copy(pattern, head_smem, sem.at[52])
    small_copies = [
        pltpu.make_async_copy(node_of, small[0], sem.at[53]),
        pltpu.make_async_copy(counts_in.at[pl.ds(0, 1)], small[1], sem.at[54]),
    ]
    for one in [pattern_copy, *small_copies]:
        one.start()
    pattern = head_smem
    cyl = lax.axis_index("cyl")
    rho = prox[0] if is_hub else prox[cyl]
    inv = jnp.broadcast_to((1.0 / (1.0 + TAU * jnp.full((8, BLK), rho, jnp.float32)))[:1], (ROWS, BLK))
    coef = TAU * inv
    pull = TAU * rho * inv

    def copy(src, dst, k):
        return pltpu.make_async_copy(src, dst, sem.at[k])

    block_copies = []
    for n in range(4):
        at = pl.ds(8 * n, 8)
        group = [copy(blocks.at[at, k], wide.at[at, :, pl.ds(k * BLK, BLK)], 40 + 3 * n + k) for k in range(3)]
        block_copies.append(group)
    dual_copy = copy(start_dual, u, 2)
    node_copy = copy(node_in, nodes, 3)
    first_copy = copy(first_in, firsts, 4)
    rhs_copy = copy(rhs, rh, 5)
    chunk_copies = []
    for n in range(NZ // CHUNK):
        at = pl.ds(n * CHUNK, CHUNK)
        where = z.at[:, at] if n * CHUNK < NNA else z_own.at[:, pl.ds(n * CHUNK - NNA, CHUNK)]
        group = [copy(costs.at[:, at], gc.at[:, at], 6 + 3 * n), copy(start.at[:, at], where, 7 + 3 * n)]
        if n * CHUNK < NNA:
            group.append(copy(mult.at[:, at], gm.at[:, at], 8 + 3 * n))
        chunk_copies.append(group)
    own_copies = sum(chunk_copies[NNA // CHUNK :], [])
    for one in [*sum(block_copies, []), dual_copy, *own_copies, first_copy]:
        one.start()
    for n, group in enumerate(chunk_copies[: NNA // CHUNK]):
        if n == N1 // CHUNK - 1:
            node_copy.start()
        for one in group:
            one.start()
    rhs_copy.start()
    if is_hub:
        own_copy = copy(own_in.at[0], extra[0], 0)
        own_copy.start()

    pattern_copy.wait()

    def clear(c, carry):
        lead_of[c] = -1
        return carry

    lax.fori_loop(0, CBA, clear, 0, unroll=16)

    def note(r, carry):
        used, dups = carry
        for k in range(2):
            c = pattern[k + 1, r]
            s = 2 * r + k
            was = lead_of[c]
            new = (was < 0).astype(jnp.int32)
            lead = jnp.where(was < 0, s, was)
            lead_of[c] = lead
            head[s] = lead
            coupled[used] = c
            slot[used] = s
            dup_to[dups] = lead
            dup_from[dups] = s
            used, dups = used + new, dups + 1 - new
        return used, dups

    used, dups = lax.fori_loop(0, RB, note, (0, 0), unroll=4)

    def place(c, unused):
        free[unused] = c
        return unused + (lead_of[c] < 0).astype(jnp.int32)

    lax.fori_loop(0, CBA, place, 0, unroll=8)

    def fill(j, carry):
        coupled[j] = free[64 + j - used]
        slot[j] = ZERO_SLOT
        return carry

    lax.fori_loop(used, 64, fill, 0)
    for one in small_copies:
        one.wait()
    counts[...] = down(small[1][...].reshape(1, ROWS))
    hot = one_hot(small[0][...])
    hot_low = hot.astype(jnp.bfloat16)[:, :NODES]
    hot_turned = hot.T[:NODES].astype(jnp.bfloat16)

    for one in (back, back_odd):
        one[:, cols(ZERO_SLOT)] = jnp.zeros((ROWS, BLK), jnp.float32)
    def arrange(r, carry):
        for k in range(3):
            tall[r, k * BLK : (k + 1) * BLK, :] = wide[r, :, k * BLK : (k + 1) * BLK].T
        return carry

    for n in range(4):
        for one in block_copies[n]:
            one.wait()
        lax.fori_loop(8 * n, 8 * n + 8, arrange, 0, unroll=8)
    for one in own_copies:
        one.wait()
    dual_copy.wait()

    def choose(live, new, old):
        return new if live is None else jnp.where(live, new, old)

    def spread(r, low, out, live):
        product = dot(low, wide[r])
        out[:, 2 * r * BLK : (2 * r + 2) * BLK] = product[:, BLK:]
        at = slice(r * BLK, (r + 1) * BLK)
        now = z_own[:, at]
        cost = gc[:, NNA + r * BLK : NNA + (r + 1) * BLK]
        fresh = jnp.clip(now + TAU * (product[:, :BLK] - cost), 0.0, 1.0)
        ext_own[:, at] = (fresh + fresh - now).astype(jnp.bfloat16)
        z_own[:, at] = choose(live, fresh, now)

    def merge(out):
        def step(k, carry):
            to = cols(dup_to[k])
            out[:, to] += out[:, cols(dup_from[k])]
            return carry

        lax.fori_loop(0, dups, step, 0)

    def loose(j, lives):
        c = cols(free[j])
        now = z[:, c]
        shift = d[:, c]
        for t in range(6):
            fresh = jnp.clip(now * inv + shift, 0.0, 1.0)
            now = fresh if t < 3 else jnp.where(lives[t - 3], fresh, now)
        z_free[:, cols(j)] = now

    def touch(before, after, back_in, live, lives, base, loose_count):
        for r in range(RB):
            for k in range(2):
                c = cols(coupled[2 * r + k])
                s = cols(slot[2 * r + k])
                now = before[:, c]
                fresh = jnp.clip(now * inv + back_in[:, s] * coef + d[:, c], 0.0, 1.0)
                ext[:, s] = (fresh + fresh - now).astype(jnp.bfloat16)
                after[:, c] = choose(live, fresh, now)
            if r < loose_count:
                loose(base + r, lives)

    def image(live):
        for r in range(RB):
            at = slice(r * BLK, (r + 1) * BLK)
            left = [ext_own[:, at], ext[:, cols(head[2 * r])], ext[:, cols(head[2 * r + 1])]]
            product = dot(jnp.concatenate(left, axis=1), tall[r])
            old = u[:, at]
            new = choose(live, jnp.maximum(0.0, old + SIGMA * (rh[:, at] - product)), old)
            u[:, at] = new
            uq[:, at] = new.astype(jnp.bfloat16)

    def turn(t, before, after, back_in, back_out, base, loose_count):
        live = counts[...] > t
        lives = [counts[...] > k for k in range(3, 6)]
        touch(before, after, back_in, live, lives, base, loose_count)
        image(live)
        next_live = counts[...] > t + 1
        for r in range(RB):
            spread(r, uq[:, r * BLK : (r + 1) * BLK], back_out, next_live)
        merge(back_out)

    def send(src, dst, k):
        one = pltpu.make_async_copy(src, dst, osem.at[k])
        one.start()
        return one

    def sum_nodes(block):
        high, low = split(z[:, cols(CB1 + block)])
        first = jnp.sum(z[:, cols(block)], axis=0, keepdims=True)
        return dot(hot_turned, high) + dot(hot_turned, low), first

    outs = []
    for r in range(RB):
        spread(r, u[:, r * BLK : (r + 1) * BLK].astype(jnp.bfloat16), back, None)
    merge(back)
    first_copy.wait()
    node_copy.wait()
    for n in range(NNA // CHUNK):
        for one in chunk_copies[n]:
            one.wait()

        def prepare(c, carry):
            if n * CHUNK < N1:
                target = jnp.broadcast_to(firsts[pl.ds(c, 1), :], (ROWS, BLK))
            else:
                high, low = split(nodes[:, cols(c - CB1)])
                target = dot(hot_low, high) + dot(hot_low, low)
            d[:, cols(c)] = pull * target - coef * (gc[:, cols(c)] + gm[:, cols(c)])
            return carry

        lax.fori_loop(n * PER, (n + 1) * PER, prepare, 0, unroll=8)
    rhs_copy.wait()

    def pair(i, carry):
        turn(2 * i, z, z_odd, back, back_odd, 16 * i, 16)
        turn(2 * i + 1, z_odd, z, back_odd, back, 0, 0)
        return carry

    lax.fori_loop(0, 2, pair, 0)
    turn(4, z, z_odd, back, back_odd, 32, 32)
    final = counts[...] > 5
    touch(z_odd, z, back_odd, final, None, 0, 0)

    def put_back(j, carry):
        z[:, cols(free[j])] = z_free[:, cols(j)]
        return carry

    lax.fori_loop(0, 64, put_back, 0, unroll=8)

    if is_hub:
        own_copy.wait()
        own = extra[0]

        def linear(c, acc):
            weight = gm[:, cols(c)] + rho * z[:, cols(c)]
            gm[:, cols(c)] = weight
            return acc + (gc[:, cols(c)] + weight) * own[:, cols(c)]

        def cost(c, acc):
            return acc + gc[:, cols(c)] * own[:, cols(c)]

        total = jnp.zeros((ROWS, BLK), jnp.float32)
        for n in range(NNA // CHUNK):
            total = lax.fori_loop(n * PER, (n + 1) * PER, linear, total, unroll=4)
            at = pl.ds(n * CHUNK, CHUNK)
            outs.append(send(gm.at[:, at], weights.at[:, at], n))
        total = lax.fori_loop(CBA, NZ // BLK, cost, total, unroll=4)
        lagrange[...] = jnp.sum(total.reshape(ROWS // 8, 8, BLK), axis=0)
    else:
        outs += [send(z, primal.at[0, :, pl.ds(0, NNA)], 0), send(z_own, primal.at[0, :, pl.ds(NNA, NZ - NNA)], 6)]
        tally = jnp.sum(hot, axis=0, keepdims=True)
        zeros = jnp.zeros((SHARD - HALF - 2, BLK), jnp.float32)

        image(final)
        outs.append(send(u, dual.at[0], 1))

        def shard(m, carry):
            for c in range(N_CYL):
                block = c * PER + m
                high, low = split(z[:, cols(CB1 + block)])
                node_sum = dot(hot_turned, high) + dot(hot_turned, low)
                first_sum = jnp.sum(z[:, cols(block)], axis=0, keepdims=True)
                tail = jnp.concatenate([first_sum, tally, zeros], axis=0)
                for half in range(2):
                    at = (2 * m + half) * N_CYL + c
                    extra[0][at, :HALF, :] = node_sum[half * HALF : (half + 1) * HALF]
                    extra[0][at, HALF:, :] = tail
            return carry

        for n in range(4):
            lax.fori_loop(4 * n, 4 * n + 4, shard, 0, unroll=4)
            at = pl.ds(GROUPS * n, GROUPS)
            outs.append(send(extra[0].at[at], sums.at[at], 2 + n))
    for one in outs:
        one.wait()


def solve(kind, *args):
    f32, bf16, i32 = jnp.float32, jnp.bfloat16, jnp.int32
    V = pltpu.VMEM
    wide, tall = (RB, BLK, 3 * BLK), (RB, 3 * BLK, BLK)
    shares = (GROUPS * N_CYL, SHARD, BLK)
    if kind == "hub":
        outs = [((ROWS, NNA), f32), ((8, BLK), f32)]
        extra, out_specs, in_more = [V((ROWS, NZ), f32)], [HBM, VM], [HBM, HBM]
    else:
        outs = [((1, ROWS, NZ), f32), ((1, ROWS, M), f32), (shares, f32)]
        extra, out_specs, in_more = [V(shares, f32)], [HBM] * 3, [HBM]
    return pl.pallas_call(
        functools.partial(solve_kernel, kind),
        out_shape=[jax.ShapeDtypeStruct(*one) for one in outs],
        in_specs=[HBM, SM, HBM, HBM] + [HBM] * 7 + in_more,
        out_specs=out_specs,
        scratch_shapes=[
            *[pltpu.SMEM((136,), i32)] * 7,
            V((ROWS, BLK), i32),
            V((ROWS, NNA), f32),
            V((ROWS, NNA), f32),
            V((ROWS, M), f32),
            V((ROWS, 64 * BLK), f32),
            V((ROWS, NNA), f32),
            V((ROWS, NZ), f32),
            V((ROWS, NNA), f32),
            V((ROWS, 65 * BLK), f32),
            V((ROWS, 65 * BLK), f32),
            V((ROWS, 65 * BLK), bf16),
            V((ROWS, M), bf16),
            V((ROWS, M), f32),
            V((ROWS, M), bf16),
            V((ROWS, M), f32),
            V(wide, bf16),
            V(tall, bf16),
            V((NODES, N2), f32),
            V((CB1, BLK), f32),
            *extra,
            V((1, ROWS), i32),
            V((1, 1, ROWS), i32),
            pltpu.SMEM((3, RB), i32),
            pltpu.SemaphoreType.DMA((60,)),
            pltpu.SemaphoreType.DMA((8,)),
        ],
        compiler_params=pltpu.CompilerParams(vmem_limit_bytes=VMEM_LIMIT),
        cost_estimate=pl.CostEstimate(flops=10**10, bytes_accessed=4 * 10**7, transcendentals=0),
        name="solve_" + kind,
    )(*args)


def average_kernel(prox, sums, lagrange, out):
    cyl = lax.axis_index("cyl")
    half = lax.axis_index("scen") % 2
    totals = [sums[c] for c in range(N_CYL)]
    for i in range(1, GROUPS):
        totals = [total + sums[i * N_CYL + c] for c, total in enumerate(totals)]
    hub = totals[0]
    tally = jnp.broadcast_to(hub[HALF + 1 : HALF + 2], (HALF, BLK))
    lanes = lax.broadcasted_iota(jnp.int32, (HALF, BLK), 1)
    wanted = lax.broadcasted_iota(jnp.int32, (HALF, BLK), 0) + half * HALF
    count = jnp.sum(jnp.where(lanes == wanted, tally, 0.0), axis=1, keepdims=True)
    low = hub[:HALF] / count
    first = hub[HALF : HALF + 1] * (1.0 / SCEN)
    once = jnp.where(half == 0, first, jnp.zeros_like(first))
    lane = lax.broadcasted_iota(jnp.int32, (1, BLK), 1)
    scalars = jnp.where(lane == cyl, jnp.sum(lagrange[...]), 0.0)
    for c, total in enumerate(totals):
        both = jnp.sum(low * total[:HALF]) + jnp.sum(once * total[HALF : HALF + 1])
        scalars = scalars - jnp.where(lane == c, prox[0] * both, 0.0)
    top = low[: SHARD // 2]
    zeros = jnp.zeros((SHARD - HALF - 2, BLK), jnp.float32)
    bottom = jnp.concatenate([low[SHARD // 2 :], first, scalars, zeros], axis=0)

    def put(i, carry):
        for c in range(N_CYL):
            out[i * N_CYL + c] = bottom if c % 2 else top
        return carry

    lax.fori_loop(0, GROUPS, put, 0, unroll=2)


def average(prox, sums, lagrange):
    return pl.pallas_call(
        average_kernel,
        out_shape=jax.ShapeDtypeStruct((GROUPS * N_CYL, SHARD // 2, BLK), jnp.float32),
        in_specs=[SM, VM, VM],
        out_specs=VM,
        compiler_params=pltpu.CompilerParams(vmem_limit_bytes=32 * 2**20),
        cost_estimate=pl.CostEstimate(flops=10**7, bytes_accessed=4 * 10**6, transcendentals=0),
        name="average",
    )(prox, sums, lagrange)


def fetch_shards(mine, other, shards, sem):
    core = lax.axis_index("cyl") % 2
    parts = [
        pltpu.make_async_copy(mine, shards.at[core], sem.at[0]),
        pltpu.make_async_copy(other, shards.at[1 - core], sem.at[1]),
    ]
    for one in parts:
        one.start()
    return parts


def averages(shards, c, m):
    lead = 2 * N_CYL * m + c
    rest = slice(0, HALF - SHARD // 2)
    pieces = [shards[0, lead], shards[1, lead, rest, :], shards[0, lead + N_CYL], shards[1, lead + N_CYL, rest, :]]
    return jnp.concatenate(pieces, axis=0), shards[1, lead, pl.ds(HALF - SHARD // 2, 1), :]


def update_kernel(
    prox, mine, other, weights, node_of, multipliers, first_out, node_out, objectives, shards, w, nodes, sem, osem
):
    rho = prox[0]
    parts = fetch_shards(mine, other, shards, sem)
    chunks = []
    for n in range(NNA // CHUNK):
        at = pl.ds(n * CHUNK, CHUNK)
        chunks.append(pltpu.make_async_copy(weights.at[:, at], w.at[:, at], sem.at[2 + n]))
        chunks[-1].start()
    hot = one_hot(node_of[...]).astype(jnp.bfloat16)[:, :NODES]
    for one in parts:
        one.wait()
    outs = []
    for n in range(NNA // CHUNK):
        chunks[n].wait()

        def step(m, carry):
            node_avg, first = averages(shards, n % N_CYL, m)
            block = (n % N_CYL) * PER + m
            if n * CHUNK < N1:
                first_out[pl.ds(block, 1), :] = first
                own = jnp.broadcast_to(first, (ROWS, BLK))
            else:
                nodes[:, cols(block)] = node_avg
                high, low = split(node_avg)
                own = dot(hot, high) + dot(hot, low)
            c = cols(n * PER + m)
            w[:, c] = w[:, c] - rho * own
            return carry

        lax.fori_loop(0, PER, step, 0, unroll=8)
        at = pl.ds(n * CHUNK, CHUNK)
        outs.append(pltpu.make_async_copy(w.at[:, at], multipliers.at[:, at], osem.at[n]))
        outs[-1].start()
        if n * CHUNK >= N1:
            at = pl.ds(n * CHUNK - N1, CHUNK)
            outs.append(pltpu.make_async_copy(nodes.at[:, at], node_out.at[:, at], osem.at[n + 4]))
            outs[-1].start()

    def add(i, acc):
        return acc + shards[1, i, 8:, :]

    total = lax.fori_loop(1, GROUPS * N_CYL, add, shards[1, 0, 8:, :], unroll=8)
    lane = lax.broadcasted_iota(jnp.int32, (1, BLK), 1)
    for c in range(N_CYL):
        objectives[c] = jnp.sum(jnp.where(lane == c, total[1:2], 0.0)) * (1.0 / SCEN)
    for one in outs:
        one.wait()


def update(prox, mine, other, weights, node_of):
    f32 = jnp.float32
    V = pltpu.VMEM
    return pl.pallas_call(
        update_kernel,
        out_shape=[
            jax.ShapeDtypeStruct((ROWS, NNA), f32),
            jax.ShapeDtypeStruct((CB1, BLK), f32),
            jax.ShapeDtypeStruct((NODES, N2), f32),
            jax.ShapeDtypeStruct((N_CYL,), f32),
        ],
        in_specs=[SM, ANY, ANY, HBM, VM],
        out_specs=[HBM, VM, HBM, SM],
        scratch_shapes=[
            V((2, GROUPS * N_CYL, SHARD // 2, BLK), f32),
            V((ROWS, NNA), f32),
            V((NODES, N2), f32),
            pltpu.SemaphoreType.DMA((12,)),
            pltpu.SemaphoreType.DMA((12,)),
        ],
        compiler_params=pltpu.CompilerParams(vmem_limit_bytes=32 * 2**20),
        cost_estimate=pl.CostEstimate(flops=10**9, bytes_accessed=2 * 10**7, transcendentals=0),
        name="update",
    )(prox, mine, other, weights, node_of)


def body(
    costs,
    rhs,
    multipliers,
    xbar_first_in,
    xbar_node_in,
    prox_weights,
    start_primal,
    start_dual,
    recourse_blocks,
    block_pattern,
    node_of,
    pdhg_counts,
):
    own_counts = pdhg_counts.reshape(1, 1, ROWS)
    all_counts = lax.all_to_all(jnp.broadcast_to(own_counts, (N_CYL, 1, ROWS)), "cyl", 0, 0, tiled=True)
    pattern = block_pattern.T
    node_row = node_of.reshape(1, ROWS)
    data = (costs, rhs, multipliers, xbar_first_in.reshape(CB1, BLK), xbar_node_in, start_primal, start_dual)
    ints = (pattern, prox_weights, node_row)
    primal, dual, sums = solve("own", *ints, own_counts, *data, recourse_blocks)
    sums, all_counts = lax.optimization_barrier((sums, all_counts))
    gathered = lax.all_to_all(sums, ALL, 0, 0, tiled=True)
    weights, lagrange = solve("hub", *ints, all_counts, *data, recourse_blocks, primal)
    shares = average(prox_weights, gathered, lagrange)
    mine = lax.all_to_all(shares, ALL, 0, 0, tiled=True)
    other = lax.ppermute(mine, "cyl", [(0, 1), (1, 0), (2, 3), (3, 2)])
    new_multipliers, first, xbar_node, objectives = update(prox_weights, mine, other, weights, node_row)
    return (primal, dual, first.reshape(N1), xbar_node, new_multipliers, objectives)


def solution(mesh):
    return jax.shard_map(
        body,
        mesh=mesh,
        in_specs=(
            P("scen", None),
            P("scen", None),
            P("scen", None),
            P(),
            P(),
            P(),
            P("scen", None),
            P("scen", None),
            P(),
            P(),
            P("scen"),
            P("cyl", "scen"),
        ),
        out_specs=(P("cyl", "scen", None), P("cyl", "scen", None), P(), P(), P("scen", None), P()),
        check_vma=False,
    )
```
